32 devices in a mesh: px: 4 (over z), pz: 8 (over y, x, core).
Axes of the slice: x: 2, y: 2, z: 4, core: 2. Of those that a mesh axis runs over, the one named last changes fastest.
Arguments:
- charge: float32 [8192, 128], P(('px', 'pz')), may hold values from -6 to 6
- dest: int32 [8192, 1], P(('px', 'pz')), may hold values from 0 to 31; in each aligned block of 256 rows (0 to 255, 256 to 511, ...) at most 16 rows name the same one
- local_ids: int32 [8192], P(('px', 'pz')), may hold values from 0 to 255
- green_hat: float32 [64, 64, 2048], P(None, 'px', 'pz'), may hold values from 0.1 to 10, as said below
Outputs:
- potential: float32 [8192, 128], P(('px', 'pz'))
The draws below stay inside these ranges and needn't reach their ends.
Inputs may be any that keep to these rules, and one draw needn't show every extreme that they name: `dest`: among the 256 slots of one box, no pencil is named by more than 16; some pencil is named by exactly 16. green_hat is even in every dimension: its value at frequencies (k1, k2, k3) equals that at ((64 - k1) mod 2 * 32, (64 - k2) mod 2 * 32, (2048 - k3) mod 2 * 1024) taken in any single dimension.
All inputs are finite; a program needn't handle non-finite values.
Results may differ from the reference program's by a relative error of at most 0.00007.
Values sent between devices are 32-bit elements; how exact they have to be, the bound alone decides.
A program may use at most 64 MiB of HBM per device.

```python
import math
import jax
import jax.numpy as jnp
import numpy as np

CXP = 8
CYP = 4
NZP = 1024
SLOTS = 256
PBLK = 256
CAP = 16
NX = 32
NY = 32
N_PX = 4
N_PZ = 8
DEVICES = 32


def mirror_mean(values, axis_number):
    length = values.shape[axis_number]
    mirrored_index = (length - jnp.arange(length, dtype=jnp.int32)) % length
    return 0.5 * (values + jnp.take(values, mirrored_index, axis=axis_number))


def draw_green_hat(key, part):
    shape = (2 * NX, 2 * NY, 2 * NZP)
    values = jax.random.uniform(key, shape, jnp.float32, 0.1, 10.0)
    values = mirror_mean(values, 0)
    values = mirror_mean(values, 1)
    values = mirror_mean(values, 2)
    return values.astype(jnp.float32)


def set_ends(drawn, key, low, top_value):
    longest = drawn.shape.index(max(drawn.shape))
    spots = []
    for shift in (0, 1):
        where = [jax.random.randint(jax.random.fold_in(key, axis), (), 0, length) for axis, length in enumerate(drawn.shape)]
        where[longest] = (where[longest] + shift) % drawn.shape[longest]
        spots.append(tuple(where))
    return drawn.at[spots[0]].set(low).at[spots[1]].set(top_value)


def level_of(rng, extent, pieces, smallest, high):
    gain = 1.0
    for axis_at, shards_of in pieces:
        draws = jax.random.uniform(jax.random.fold_in(jax.random.fold_in(rng, 6), axis_at), (shards_of,), jnp.float32, smallest / len(pieces), high / len(pieces))
        gain = gain * jnp.repeat(jnp.exp(draws), extent[axis_at] // shards_of).reshape((-1,) + (1,) * (len(extent) - 1 - axis_at))
    return gain


def shared_out(key, own, number, rows, count, top, most, skew):
    order = jax.random.permutation(key, count)
    heavy_load, ordinary = shares(count, rows * top, most, skew, True), shares(count, rows * top, most, skew, False)
    places = jnp.arange(count)

    def named(lengths, rotation):
        used = int((lengths > 0).sum())
        fixed = max(1, used // 4)
        moved = fixed + (places - fixed + rotation * (used - fixed)) % max(1, count - fixed)
        return jnp.zeros((count,), jnp.int32).at[order[jnp.where(places < fixed, places, moved)]].set(jnp.asarray(lengths, jnp.int32))

    lengths = jnp.where(number % 4 == 0, named(heavy_load, number // 4), named(ordinary, number - number // 4 - 1))
    mixed = jax.random.permutation(jax.random.fold_in(own, 3), count)
    donor, taker = mixed[0:count // 2 * 2:2], mixed[1:count // 2 * 2:2]
    room = jnp.minimum(lengths[donor] - 1, most - lengths[taker]) // 2
    room = jnp.where((donor == order[0]) | (taker == order[0]) | (lengths[taker] == 0), 0, jnp.maximum(room, 0))
    moved = jax.random.randint(jax.random.fold_in(own, 4), (count // 2,), 0, 1 << 20) % (room + 1)
    lengths = lengths.at[donor].add(-moved).at[taker].add(moved)
    items = jnp.searchsorted(jnp.cumsum(lengths), jnp.arange(rows * top), side="right").astype(jnp.int32)
    listing = items.reshape(top, rows).T
    listing = listing[jax.random.permutation(jax.random.fold_in(own, 1), rows)]
    rotation = jax.random.randint(jax.random.fold_in(own, 2), (rows, 1), 0, top)
    return jnp.take_along_axis(listing, (jnp.arange(top)[None, :] + rotation) % top, axis=1)


def shares(count, total, limit, skew, full):
    weights = [(1 << 20) // math.isqrt(grade ** skew) + 1 for grade in range(1, count + 1)]
    largest = limit if full else min(limit, max(-(-total // count), total * weights[0] // sum(weights)))
    least = 1 if total - largest >= count - 1 else 0
    holding, surplus = [largest] + [least] * (count - 1), total - largest - least * (count - 1)
    while surplus > 0:
        free = [i for i in range(1, count) if holding[i] < largest] or [i for i in range(1, count) if holding[i] < limit]
        mass, budget = sum([weights[i] for i in free]), surplus
        for i in free:
            extra = min(limit - holding[i], max(1, budget * weights[i] // mass), surplus)
            holding[i] = holding[i] + extra
            surplus = surplus - extra
    return np.array(holding)


def noise(stream_key, dims, scale, bound, pieces=(), held_as=jnp.bfloat16):
    drawn = jax.random.normal(stream_key, dims, jnp.float32) * scale
    if len(pieces) > 0:
        drawn = level_of(stream_key, dims, pieces, -0.22, 0.18) * drawn
    return jnp.clip(drawn, min=-bound, max=bound).astype(held_as)


def setup_inputs(seed: int = 0) -> dict:
    key_of = jax.random.split(jax.random.key(seed), 5)
    charge = noise(key_of[0], (DEVICES * SLOTS, 128), 1.0, 6.0, ((0, 32),), jnp.float32)
    dest_keys = jax.random.split(jax.random.fold_in(key_of[1], 1), (DEVICES * SLOTS) // SLOTS)
    dest_turns = jax.random.permutation(jax.random.fold_in(key_of[1], 3), (DEVICES * SLOTS) // SLOTS)
    dest = jax.vmap(lambda own, number: shared_out(jax.random.fold_in(key_of[1], 2), own, number, SLOTS, DEVICES, 1, CAP, 2))(dest_keys, dest_turns).reshape((DEVICES * SLOTS, 1))
    local_ids = set_ends(jax.random.randint(key_of[2], (DEVICES * SLOTS,), 0, PBLK), jax.random.fold_in(key_of[2], 1), 0, PBLK - 1).astype(jnp.int32)
    green_hat = draw_green_hat(jax.random.fold_in(key_of[4], 71), 0)
    return dict(charge=charge, dest=dest, local_ids=local_ids, green_hat=green_hat)


def reference(charge, dest, local_ids, green_hat):
    wide_x = CXP * N_PX
    wide_y = CYP * N_PZ
    target = dest[:, 0] * PBLK + local_ids
    blocks = jax.ops.segment_sum(charge, target, num_segments=DEVICES * PBLK)
    grid = blocks.reshape(N_PX, N_PZ, CXP, CYP, NZP).transpose(0, 2, 1, 3, 4).reshape(wide_x, wide_y, NZP)
    padded = jnp.zeros((2 * wide_x, 2 * wide_y, 2 * NZP), jnp.float32).at[:wide_x, :wide_y, :NZP].set(grid)
    spectrum = jnp.fft.fftn(padded)
    phi = jnp.real(jnp.fft.ifftn(spectrum * green_hat))[:wide_x, :wide_y, :NZP].astype(jnp.float32)
    back = phi.reshape(N_PX, CXP, N_PZ, CYP, NZP).transpose(0, 2, 1, 3, 4).reshape(DEVICES * PBLK, 128)
    return back[target]
```

```python
import math

import jax
import jax.numpy as jnp
import numpy as np
from jax import lax
from jax.sharding import PartitionSpec as P

CXP = 8
CYP = 4
NZP = 1024
AXES = ("px", "pz")


def split_table(table):
    high = table.astype(np.float32).astype(jnp.bfloat16)
    low = (table - high.astype(np.float64)).astype(np.float32).astype(jnp.bfloat16)
    return np.asarray(high), np.asarray(low)


def long_table():
    n = np.arange(NZP)[:, None]
    k = np.arange(2 * NZP)[None, :]
    angle = (n * k % (2 * NZP)) * (2.0 * math.pi / (2 * NZP))
    return np.cos(angle) + np.sin(angle)


def short_tables(wide, frequencies):
    period = 2 * wide
    folded = np.minimum(frequencies, period - frequencies)
    angle = (frequencies[:, None] * np.arange(wide)[None, :] % period) * (2.0 * math.pi / period)
    table = np.concatenate((np.cos(angle), np.sin(angle)), axis=0)
    weight = np.where((folded == 0) | (folded == wide), 1.0, 2.0) / period
    count = np.array([(folded == f).sum() for f in folded])
    weight = np.tile(weight / count, 2)
    return table, table * weight[:, None]


def split(values):
    high = lax.reduce_precision(values, 8, 7)
    return high.astype(jnp.bfloat16), (values - high).astype(jnp.bfloat16)


def product(form, values, table):
    high, low = split(values)
    t_high, t_low = table
    dot = lambda a, b: jnp.einsum(form, a, b, preferred_element_type=jnp.float32)
    return dot(high, t_high) + (dot(low, t_high) + dot(high, t_low))


def pick(form, one_hot, values):
    high, low = split(values)
    dot = lambda b: jnp.einsum(form, one_hot, b, preferred_element_type=jnp.float32)
    return dot(high) + dot(low)


def kept_frequencies(wide_y, n_px):
    own = 2 * wide_y // n_px
    return (np.arange(n_px)[:, None] * own + np.arange(own // 2 + 1)[None, :]).reshape(-1)


def local(charge, dest, local_ids, green_hat):
    n_px = lax.axis_size("px")
    n_pz = lax.axis_size("pz")
    n_dev = n_px * n_pz
    wide_x, wide_y = CXP * n_px, CYP * n_pz
    slots = charge.shape[0]
    cap = 2 * slots // n_dev
    pencil_blocks = CXP * CYP * NZP // 128
    own = 2 * wide_y // n_px
    group = 2 * NZP // n_dev

    green = lax.all_to_all(
        green_hat[: wide_x + 1, : own // 2 + 1], "px", split_axis=2, concat_axis=1, tiled=True
    )

    route = dest[:, 0]
    named = (route[:, None] == jnp.arange(n_dev)[None, :]).astype(jnp.bfloat16)
    before = jnp.asarray(np.tril(np.ones((slots, slots)), -1), jnp.bfloat16)
    rank = jnp.sum(
        jnp.einsum("st,td->sd", before, named, preferred_element_type=jnp.float32) * named, axis=1
    ).astype(jnp.int32)
    place = route * cap + rank
    packing = (place[:, None] == jnp.arange(n_dev * cap)[None, :]).astype(jnp.bfloat16)
    sent = pick("sr,sl->rl", packing, charge).reshape(n_dev, cap, 128)
    ids = jnp.einsum(
        "sr,s->r", packing, (local_ids + 1).astype(jnp.bfloat16), preferred_element_type=jnp.float32
    ).reshape(n_dev, 1, cap)
    sent = jnp.concatenate((sent, jnp.pad(ids, ((0, 0), (0, 0), (0, 128 - cap)))), axis=1)
    got = lax.all_to_all(sent, AXES, split_axis=0, concat_axis=0, tiled=True)
    ids = got[:, cap, :cap].reshape(n_dev * cap).astype(jnp.int32) - 1
    placing = (ids[:, None] == jnp.arange(pencil_blocks)[None, :]).astype(jnp.bfloat16)
    field = pick("rb,rl->bl", placing, got[:, :cap].reshape(n_dev * cap, 128))
    field = field.reshape(CXP * CYP, NZP)

    long = split_table(long_table())
    spectrum = product("pz,zk->pk", field, long)
    spectrum = spectrum.reshape(CXP * CYP, n_pz, n_px, group).transpose(2, 1, 0, 3)
    spectrum = spectrum.reshape(n_dev, CXP * CYP, group)
    turned = lax.all_to_all(spectrum, AXES, split_axis=0, concat_axis=0, tiled=True)
    planes = turned.reshape(n_px, n_pz, CXP, CYP, group).transpose(0, 2, 1, 3, 4)
    planes = planes.reshape(wide_x, wide_y, group)

    kept_y = kept_frequencies(wide_y, n_px)
    y_table, y_back = short_tables(wide_y, kept_y)
    x_table, x_back = short_tables(wide_x, np.arange(wide_x + 1))
    planes = product("xyk,qy->xqk", planes, split_table(y_table))
    planes = product("xqk,ux->uqk", planes, split_table(x_table))
    count_x, count_y = wide_x + 1, len(kept_y)
    planes = planes.reshape(2, count_x, 2, count_y, group) * green[None, :, None]
    planes = planes.reshape(2 * count_x, 2 * count_y, group)
    planes = product("uqk,ux->xqk", planes, split_table(x_back))
    planes = product("xqk,qy->xyk", planes, split_table(y_back))

    planes = planes.reshape(n_px, CXP, n_pz, CYP, group).transpose(0, 2, 1, 3, 4)
    planes = planes.reshape(n_dev, CXP * CYP, group)
    turned = lax.all_to_all(planes, AXES, split_axis=0, concat_axis=0, tiled=True)
    spectrum = turned.reshape(n_px, n_pz, CXP * CYP, group).transpose(2, 1, 0, 3)
    spectrum = spectrum.reshape(CXP * CYP, 2 * NZP)
    phi = product("pk,zk->pz", spectrum, long) * (1.0 / (2 * NZP))
    back = pick("rb,bl->rl", placing, phi.reshape(pencil_blocks, 128)).reshape(n_dev, cap, 128)
    got = lax.all_to_all(back, AXES, split_axis=0, concat_axis=0, tiled=True)
    return pick("sr,rl->sl", packing, got.reshape(n_dev * cap, 128))


def solution(mesh):
    return jax.shard_map(
        local,
        mesh=mesh,
        in_specs=(
            P(AXES, None),
            P(AXES, None),
            P(AXES),
            P(None, "px", "pz"),
        ),
        out_specs=P(AXES, None),
        check_vma=False,
    )
```

```python
import functools
import math

import jax
import jax.numpy as jnp
import numpy as np
from jax import lax
from jax.experimental import pallas as pl
from jax.experimental.pallas import tpu as pltpu
from jax.sharding import PartitionSpec as P

CXP = 8
CYP = 4
NZP = 1024
AXES = ("px", "pz")


def split_table(table):
    high = table.astype(np.float32).astype(jnp.bfloat16)
    low = (table - high.astype(np.float64)).astype(np.float32).astype(jnp.bfloat16)
    return np.asarray(high), np.asarray(low)


def long_table():
    n = np.arange(NZP)[:, None]
    k = np.arange(2 * NZP)[None, :]
    angle = (n * k % (2 * NZP)) * (2.0 * math.pi / (2 * NZP))
    return np.cos(angle) + np.sin(angle)


def short_tables(wide, frequencies):
    period = 2 * wide
    folded = np.minimum(frequencies, period - frequencies)
    angle = (frequencies[:, None] * np.arange(wide)[None, :] % period) * (2.0 * math.pi / period)
    table = np.concatenate((np.cos(angle), np.sin(angle)), axis=0)
    weight = np.where((folded == 0) | (folded == wide), 1.0, 2.0) / period
    count = np.array([(folded == f).sum() for f in folded])
    weight = np.tile(weight / count, 2)
    return table, table * weight[:, None]


def split(values):
    high = lax.reduce_precision(values, 8, 7)
    return high.astype(jnp.bfloat16), (values - high).astype(jnp.bfloat16)


def product(form, values, table):
    high, low = split(values)
    t_high, t_low = table
    dot = lambda a, b: jnp.einsum(form, a, b, preferred_element_type=jnp.float32)
    return dot(high, t_high) + (dot(low, t_high) + dot(high, t_low))


def pick(form, one_hot, values):
    high, low = split(values)
    dot = lambda b: jnp.einsum(form, one_hot, b, preferred_element_type=jnp.float32)
    return dot(high) + dot(low)


def kept_frequencies(wide_y, n_px):
    own = 2 * wide_y // n_px
    return (np.arange(n_px)[:, None] * own + np.arange(own // 2 + 1)[None, :]).reshape(-1)


def local(charge, dest, local_ids, green_hat):
    n_px = lax.axis_size("px")
    n_pz = lax.axis_size("pz")
    n_dev = n_px * n_pz
    wide_x, wide_y = CXP * n_px, CYP * n_pz
    slots = charge.shape[0]
    cap = 2 * slots // n_dev
    pencil_blocks = CXP * CYP * NZP // 128
    own = 2 * wide_y // n_px
    group = 2 * NZP // n_dev

    green = lax.all_to_all(
        green_hat[: wide_x + 1, : own // 2 + 1], "px", split_axis=2, concat_axis=1, tiled=True
    )

    route = dest[:, 0]
    named = (route[:, None] == jnp.arange(n_dev)[None, :]).astype(jnp.bfloat16)
    before = jnp.asarray(np.tril(np.ones((slots, slots)), -1), jnp.bfloat16)
    rank = jnp.sum(
        jnp.einsum("st,td->sd", before, named, preferred_element_type=jnp.float32) * named, axis=1
    ).astype(jnp.int32)
    place = route * cap + rank
    packing = (place[:, None] == jnp.arange(n_dev * cap)[None, :]).astype(jnp.bfloat16)
    sent = pick("sr,sl->rl", packing, charge).reshape(n_dev, cap, 128)
    ids = jnp.einsum(
        "sr,s->r", packing, (local_ids + 1).astype(jnp.bfloat16), preferred_element_type=jnp.float32
    ).reshape(n_dev, 1, cap)
    sent = jnp.concatenate((sent, jnp.pad(ids, ((0, 0), (0, 0), (0, 128 - cap)))), axis=1)
    got = lax.all_to_all(sent, AXES, split_axis=0, concat_axis=0, tiled=True)
    ids = got[:, cap, :cap].reshape(n_dev * cap).astype(jnp.int32) - 1
    placing = (ids[:, None] == jnp.arange(pencil_blocks)[None, :]).astype(jnp.bfloat16)
    field = pick("rb,rl->bl", placing, got[:, :cap].reshape(n_dev * cap, 128))
    field = field.reshape(CXP * CYP, NZP)

    long = split_table(long_table())
    spectrum = product("pz,zk->pk", field, long)
    spectrum = spectrum.reshape(CXP * CYP, n_pz, n_px, group).transpose(2, 1, 0, 3)
    spectrum = spectrum.reshape(n_dev, CXP * CYP, group)
    turned = lax.all_to_all(spectrum, AXES, split_axis=0, concat_axis=0, tiled=True)
    planes = turned.reshape(n_px, n_pz, CXP, CYP, group).transpose(0, 2, 1, 3, 4)
    planes = planes.reshape(wide_x, wide_y, group)

    kept_y = kept_frequencies(wide_y, n_px)
    y_table, y_back = short_tables(wide_y, kept_y)
    x_table, x_back = short_tables(wide_x, np.arange(wide_x + 1))
    planes = product("xyk,qy->xqk", planes, split_table(y_table))
    planes = product("xqk,ux->uqk", planes, split_table(x_table))
    count_x, count_y = wide_x + 1, len(kept_y)
    planes = planes.reshape(2, count_x, 2, count_y, group) * green[None, :, None]
    planes = planes.reshape(2 * count_x, 2 * count_y, group)
    planes = product("uqk,ux->xqk", planes, split_table(x_back))
    planes = product("xqk,qy->xyk", planes, split_table(y_back))

    planes = planes.reshape(n_px, CXP, n_pz, CYP, group).transpose(0, 2, 1, 3, 4)
    planes = planes.reshape(n_dev, CXP * CYP, group)
    turned = lax.all_to_all(planes, AXES, split_axis=0, concat_axis=0, tiled=True)
    spectrum = turned.reshape(n_px, n_pz, CXP * CYP, group).transpose(2, 1, 0, 3)
    spectrum = spectrum.reshape(CXP * CYP, 2 * NZP)
    phi = product("pk,zk->pz", spectrum, long) * (1.0 / (2 * NZP))
    back = pick("rb,bl->rl", placing, phi.reshape(pencil_blocks, 128)).reshape(n_dev, cap, 128)
    got = lax.all_to_all(back, AXES, split_axis=0, concat_axis=0, tiled=True)
    return pick("sr,rl->sl", packing, got.reshape(n_dev * cap, 128))


LANES = 128
GROUP = 64
KEPT = 8
HALF = 32
WIDE = 32
MESH = pl.DeviceIdType.MESH


def unit_rows(frequencies, is_sine, wide):
    period = 2 * wide
    angle = (frequencies[:, None] * np.arange(wide)[None, :] % period) * (2.0 * math.pi / period)
    weight = np.where((frequencies == 0) | (frequencies == wide), 1.0, 2.0) / period
    return np.where(is_sine[:, None], np.sin(angle), np.cos(angle)) * np.sqrt(weight)[:, None]


def plane_tables(n_px, n_pz):
    starts = np.array([0, 16, 33, 49])
    raw = (starts[:, None] + np.arange(KEPT)[None, :]).reshape(-1)
    folded = np.minimum(raw, 2 * WIDE - raw)
    frequencies = np.concatenate((folded, np.where(folded == 0, WIDE, folded)))
    sine = np.concatenate((np.zeros(HALF, bool), folded != 0))
    rows = unit_rows(frequencies, sine, WIDE).reshape(2 * n_px, KEPT, n_pz, CYP)
    eye_i, eye_a = np.eye(n_px), np.eye(4)
    y_table = np.einsum("gqjb,iI,aA->ijabgIqA", rows, eye_i, eye_a)
    y_table = y_table.reshape(n_px * n_pz * 16, 2 * n_px * n_px * KEPT * 4)
    base = np.arange(HALF)
    frequencies = np.concatenate((base, np.where(base == 0, WIDE, base)))
    sine = np.concatenate((np.zeros(HALF, bool), base != 0))
    rows = unit_rows(frequencies, sine, WIDE).reshape(2 * HALF, n_px, 2, 4)
    x_table = np.einsum("uiha,qQ->hiqauQ", rows, np.eye(KEPT))
    x_table = x_table.reshape(2 * n_px * KEPT * 4, 2 * HALF * KEPT)
    return y_table, x_table


def halves(values):
    high = values.astype(jnp.bfloat16)
    return high, (values - high.astype(jnp.float32)).astype(jnp.bfloat16)


def mm(a, b, contract=((1,), (0,))):
    return lax.dot_general(a, b, (contract, ((), ())), preferred_element_type=jnp.float32)


def mm_left(values, high, low, contract=((1,), (0,))):
    v_high, v_low = halves(values)
    rows = values.shape[0]
    both = mm(jnp.concatenate((v_high, v_low), axis=0), high, contract)
    return both[:rows] + (both[rows:] + mm(v_high, low, contract))


def mm_pick(one_hot, values):
    high, low = halves(values)
    return mm(one_hot, high) + mm(one_hot, low)


def iota(shape, axis):
    return lax.broadcasted_iota(jnp.int32, shape, axis)


def as_row(column):
    return jnp.transpose(jnp.broadcast_to(column, (column.shape[0], LANES)))[0:1, :]


def as_column(row):
    return jnp.transpose(jnp.broadcast_to(row, (LANES, row.shape[1])))[:, 0:1]


def one(mask):
    return jnp.where(mask, 1.0, 0.0).astype(jnp.bfloat16)


def fused(
    n_px, n_pz, charge_ref, dest_ref, ids_ref, green_hbm, zh_hbm, zl_hbm, yh_hbm, yl_hbm, xh_hbm,
    xl_hbm, out_ref, green, zh, zl, yh, yl, xh, xl, ids_send, ids_recv, charge_send, charge_recv,
    green_send, green_recv, spec_send, spec_recv, back_send, back_recv, out_send, out_recv, scale,
    load_sems, send_sems, recv_sems
):
    n_dev = n_px * n_pz
    mi, mj = lax.axis_index("px"), lax.axis_index("pz")
    me = mi * n_pz + mj
    slots = charge_ref.shape[0]
    cap = charge_send.shape[1]
    rows = n_dev * cap
    blocks = CXP * CYP * NZP // LANES

    barrier = pltpu.get_barrier_semaphore()

    def greet(step, carry):
        peer = lax.rem(me + step, n_dev)
        pl.semaphore_signal(
            barrier, inc=1, device_id=(peer // n_pz, lax.rem(peer, n_pz)), device_id_type=MESH
        )
        return carry

    lax.fori_loop(1, n_dev, greet, 0)

    loads = [
        pltpu.make_async_copy(source, target, load_sems.at[number])
        for number, (source, target) in enumerate((
            (green_hbm.at[pl.ds(0, 40)], green), (zh_hbm, zh), (zl_hbm, zl), (yh_hbm, yh),
            (yl_hbm, yl), (xh_hbm, xh), (xl_hbm, xl),
        ))
    ]
    for load in loads:
        load.start()

    def block_copy(send, recv, number, peer):
        return pltpu.make_async_remote_copy(
            src_ref=send.at[peer],
            dst_ref=recv.at[me],
            send_sem=send_sems.at[number],
            recv_sem=recv_sems.at[number],
            device_id=(peer // n_pz, lax.rem(peer, n_pz)),
            device_id_type=MESH,
        )

    def send_all(send, recv, number):
        def body(step, carry):
            block_copy(send, recv, number, lax.rem(me + step, n_dev)).start()
            return carry

        lax.fori_loop(1, n_dev, body, 0)
        recv[me] = send[me]

    def all_of(send, recv, number, count):
        return pltpu.make_async_remote_copy(
            src_ref=send.at[pl.ds(0, count)],
            dst_ref=recv.at[pl.ds(0, count)],
            send_sem=send_sems.at[number],
            recv_sem=recv_sems.at[number],
            device_id=(mi, mj),
            device_id_type=MESH,
        )

    dest = dest_ref[...]
    named = one(dest == iota((slots, LANES), 1))
    before = one(iota((slots, slots), 1) < iota((slots, slots), 0))
    rank = jnp.sum(mm(before, named) * named.astype(jnp.float32), axis=1, keepdims=True)
    place = dest.astype(jnp.float32) * cap + rank
    ids = ids_ref[...].astype(jnp.float32) + 1.0
    dest_row = as_row(dest.astype(jnp.float32))
    owned = jnp.where(dest_row == iota((n_dev, slots), 0).astype(jnp.float32), ids, 0.0)
    ranked = one(rank == iota((slots, LANES), 1).astype(jnp.float32))
    ids_send[...] = mm(owned.astype(jnp.bfloat16), ranked).reshape(n_dev, 1, LANES)
    packing = one(as_row(place) == iota((rows, slots), 0).astype(jnp.float32))
    charge_send[...] = mm_pick(packing, charge_ref[...]).reshape(n_dev, cap, LANES)
    pl.semaphore_wait(barrier, n_dev - 1)
    send_all(ids_send, ids_recv, 0)
    send_all(charge_send, charge_recv, 1)

    loads[0].wait()
    shifted = mi >= n_px // 2
    kept = jnp.where(shifted, green[0:33, 1:9, :], green[0:33, 0:8, :])
    wide = jnp.transpose(kept[0:HALF].reshape(HALF * KEPT, 256))
    edge = green[0:40, 0, :]
    edge = jnp.concatenate((kept[HALF], edge, jnp.zeros((LANES - 48, 256), jnp.float32)), axis=0)
    green_send[...] = jnp.concatenate((wide, jnp.transpose(edge)), axis=1).reshape(n_px, GROUP, 384)

    def green_copy(target):
        return pltpu.make_async_remote_copy(
            src_ref=green_send.at[target],
            dst_ref=green_recv.at[mi],
            send_sem=send_sems.at[2],
            recv_sem=recv_sems.at[2],
            device_id=(target, mj),
            device_id_type=MESH,
        )

    for step in range(1, n_px):
        green_copy(lax.rem(mi + step, n_px)).start()
    green_recv[mi] = green_send[mi]

    all_of(ids_send, ids_recv, 0, n_dev - 1).wait_recv()
    line = iota((rows, n_dev), 0)
    spread = mm(one(line // cap == iota((rows, n_dev), 1)), ids_recv[...].reshape(n_dev, LANES).astype(jnp.bfloat16))
    own_lane = iota((rows, LANES), 1) == lax.rem(iota((rows, LANES), 0), cap)
    ids = jnp.sum(jnp.where(own_lane, spread, 0.0), axis=1, keepdims=True)
    lines = CXP * CYP

    def target_of(index):
        return (lax.rem(index, lines) * (NZP // LANES) + index // lines + 1).astype(jnp.float32)

    taking = one(ids == target_of(iota((rows, blocks), 1)))
    placing = one(as_row(ids) == target_of(iota((blocks, rows), 0)))
    all_of(charge_send, charge_recv, 1, n_dev - 1).wait_recv()
    field = mm_pick(placing, charge_recv[...].reshape(rows, LANES))
    field = jnp.concatenate([field[lines * c : lines * (c + 1)] for c in range(NZP // LANES)], axis=1)

    f_high, f_low = halves(field)
    f_both = jnp.concatenate((f_high, f_low), axis=0)
    loads[1].wait()
    loads[2].wait()
    first = iota((lines // 2, LANES), 1) < GROUP

    def forward(step, carry):
        j = lax.rem(mj + step, n_pz)
        columns = pl.ds(pl.multiple_of(j * 256, 256), 256)
        both = mm(f_both, zh[:, columns])
        total = both[:lines] + (both[lines:] + mm(f_high, zl[:, columns]))
        for pair in range(2):
            tile = total[:, pair * LANES : (pair + 1) * LANES]
            low, high = tile[: lines // 2], tile[lines // 2 :]
            low_turned, high_turned = pltpu.roll(low, GROUP, 1), pltpu.roll(high, GROUP, 1)
            spec_send[2 * pair * n_pz + j] = jnp.where(first, low, high_turned)
            spec_send[(2 * pair + 1) * n_pz + j] = jnp.where(first, low_turned, high)
        for turn in range(n_px):
            peer = lax.rem(mi + turn, n_px) * n_pz + j

            @pl.when(peer != me)
            def _():
                block_copy(spec_send, spec_recv, 3, peer).start()

        return carry

    lax.fori_loop(0, n_pz, forward, 0)
    spec_recv[me] = spec_send[me]

    all_of(green_send, green_recv, 2, n_px - 1).wait_recv()
    lane = iota((GROUP, 256), 1)
    source, target = iota((LANES, 512), 0), iota((LANES, 512), 1)
    wanted = jnp.where(target == 256, HALF, lax.rem(target, 256) // KEPT) + KEPT
    picking = one((source == wanted) & (lax.rem(target, KEPT) == 0))
    e_high, e_low = halves(green_recv[2, :, 256:384])
    e_rest = (green_recv[2, :, 256:384] - e_high.astype(jnp.float32) - e_low.astype(jnp.float32)).astype(jnp.bfloat16)
    nyquist = mm(e_high, picking) + (mm(e_low, picking) + mm(e_rest, picking))
    for i in range(n_px):
        wide = green_recv[i, :, 0:256]
        edge = jnp.concatenate((green_recv[i, :, 256:384], wide[:, LANES:]), axis=1)
        full = jnp.concatenate((wide, jnp.where(lane < KEPT, edge, wide)), axis=1)
        scale[i * GROUP : (i + 1) * GROUP, :] = full
        if i == 0:
            full = jnp.where(lax.rem(iota((GROUP, 512), 1), KEPT) == 0, nyquist, full)
        scale[(n_px + i) * GROUP : (n_px + i + 1) * GROUP, :] = full

    for load in loads[3:]:
        load.wait()
    all_of(spec_send, spec_recv, 3, n_dev - 1).wait_recv()
    planes = jnp.transpose(spec_recv[...].reshape(n_dev * 16, LANES))
    planes = mm_left(planes, yh[...], yl[...])
    groups = 2 * n_px
    planes = jnp.concatenate(
        [
            jnp.concatenate(
                [planes[h * GROUP : (h + 1) * GROUP, g * LANES : (g + 1) * LANES] for h in range(2)], axis=1
            )
            for g in range(groups)
        ],
        axis=0,
    )
    planes = mm_left(planes, xh[...], xl[...]) * scale[...]
    planes = mm_left(planes, xh[...], xl[...], ((1,), (1,)))
    planes = jnp.concatenate(
        [
            jnp.concatenate(
                [planes[g * GROUP : (g + 1) * GROUP, h * LANES : (h + 1) * LANES] for g in range(groups)], axis=1
            )
            for h in range(2)
        ],
        axis=0,
    )
    p_high, p_low = halves(planes)
    right = ((1,), (1,))
    planes = mm(yh[...], p_high, right) + (mm(yh[...], p_low, right) + mm(yl[...], p_high, right))
    back_send[...] = planes.reshape(n_dev, 16, LANES)
    send_all(back_send, back_recv, 4)

    all_of(back_send, back_recv, 4, n_dev - 1).wait_recv()
    pieces = []
    for j in range(n_pz):
        for pair in range(2):
            left, other = back_recv[2 * pair * n_pz + j], back_recv[(2 * pair + 1) * n_pz + j]
            low = jnp.where(first, left, pltpu.roll(other, GROUP, 1))
            high = jnp.where(first, pltpu.roll(left, GROUP, 1), other)
            pieces.append(jnp.concatenate((low, high), axis=0))
    phi = mm_left(jnp.concatenate(pieces, axis=1), zh[...], zl[...], right)
    phi = jnp.concatenate([phi[:, c * LANES : (c + 1) * LANES] for c in range(NZP // LANES)], axis=0)
    out_send[...] = mm_pick(taking, phi).reshape(n_dev, cap, LANES)
    send_all(out_send, out_recv, 5)
    unpacking = one(place == iota((slots, rows), 1).astype(jnp.float32))
    all_of(out_send, out_recv, 5, n_dev - 1).wait_recv()
    out_ref[...] = mm_pick(unpacking, out_recv[...].reshape(rows, LANES))

    all_of(ids_send, ids_recv, 0, n_dev - 1).wait_send()
    all_of(charge_send, charge_recv, 1, n_dev - 1).wait_send()
    all_of(green_send, green_recv, 2, n_px - 1).wait_send()
    all_of(spec_send, spec_recv, 3, n_dev - 1).wait_send()
    all_of(back_send, back_recv, 4, n_dev - 1).wait_send()
    all_of(out_send, out_recv, 5, n_dev - 1).wait_send()


def local_fused(charge, dest, local_ids, green_hat):
    n_px, n_pz = lax.axis_size("px"), lax.axis_size("pz")
    n_dev = n_px * n_pz
    slots = charge.shape[0]
    cap = 2 * slots // n_dev
    y_table, x_table = plane_tables(n_px, n_pz)
    tables = [
        piece
        for table in (long_table() / math.sqrt(2 * NZP), y_table, x_table)
        for piece in split_table(table)
    ]
    exchange = lambda lead, rows: [pltpu.VMEM((lead, rows, LANES), jnp.float32)] * 2
    vmem, anywhere = pl.BlockSpec(memory_space=pltpu.VMEM), pl.BlockSpec(memory_space=pl.ANY)
    return pl.pallas_call(
        functools.partial(fused, n_px, n_pz),
        out_shape=jax.ShapeDtypeStruct(charge.shape, jnp.float32),
        in_specs=[vmem] * 3 + [anywhere] * 7,
        out_specs=vmem,
        scratch_shapes=[
            pltpu.VMEM((40,) + green_hat.shape[1:], jnp.float32),
            *[pltpu.VMEM(table.shape, jnp.bfloat16) for table in tables],
            *exchange(n_dev, 1),
            *exchange(n_dev, cap),
            *[pltpu.VMEM((n_px, GROUP, 384), jnp.float32)] * 2,
            *exchange(n_dev, 16),
            *exchange(n_dev, 16),
            *exchange(n_dev, cap),
            pltpu.VMEM((2 * n_px * GROUP, 2 * HALF * KEPT), jnp.float32),
            pltpu.SemaphoreType.DMA((7,)),
            pltpu.SemaphoreType.DMA((6,)),
            pltpu.SemaphoreType.DMA((6,)),
        ],
        compiler_params=pltpu.CompilerParams(
            collective_id=0, has_side_effects=True, vmem_limit_bytes=48 * 1024 * 1024
        ),
    )(charge, dest, local_ids.reshape(1, slots), green_hat, *tables)


def solution(mesh):
    planes = mesh.shape["px"] == 4 and mesh.shape["pz"] == 8
    return jax.shard_map(
        local_fused if planes else local,
        mesh=mesh,
        in_specs=(
            P(AXES, None),
            P(AXES, None),
            P(AXES),
            P(None, "px", "pz"),
        ),
        out_specs=P(AXES, None),
        check_vma=False,
    )
```

```python
import functools
import math

import jax
import jax.numpy as jnp
import numpy as np
from jax import lax
from jax.experimental import pallas as pl
from jax.experimental.pallas import tpu as pltpu
from jax.sharding import PartitionSpec as P

CXP = 8
CYP = 4
NZP = 1024
AXES = ("px", "pz")


def split_table(table):
    high = table.astype(np.float32).astype(jnp.bfloat16)
    low = (table - high.astype(np.float64)).astype(np.float32).astype(jnp.bfloat16)
    return np.asarray(high), np.asarray(low)


def long_table():
    n = np.arange(NZP)[:, None]
    k = np.arange(2 * NZP)[None, :]
    angle = (n * k % (2 * NZP)) * (2.0 * math.pi / (2 * NZP))
    return np.cos(angle) + np.sin(angle)


def short_tables(wide, frequencies):
    period = 2 * wide
    folded = np.minimum(frequencies, period - frequencies)
    angle = (frequencies[:, None] * np.arange(wide)[None, :] % period) * (2.0 * math.pi / period)
    table = np.concatenate((np.cos(angle), np.sin(angle)), axis=0)
    weight = np.where((folded == 0) | (folded == wide), 1.0, 2.0) / period
    count = np.array([(folded == f).sum() for f in folded])
    weight = np.tile(weight / count, 2)
    return table, table * weight[:, None]


def split(values):
    high = lax.reduce_precision(values, 8, 7)
    return high.astype(jnp.bfloat16), (values - high).astype(jnp.bfloat16)


def product(form, values, table):
    high, low = split(values)
    t_high, t_low = table
    dot = lambda a, b: jnp.einsum(form, a, b, preferred_element_type=jnp.float32)
    return dot(high, t_high) + (dot(low, t_high) + dot(high, t_low))


def pick(form, one_hot, values):
    high, low = split(values)
    dot = lambda b: jnp.einsum(form, one_hot, b, preferred_element_type=jnp.float32)
    return dot(high) + dot(low)


def kept_frequencies(wide_y, n_px):
    own = 2 * wide_y // n_px
    return (np.arange(n_px)[:, None] * own + np.arange(own // 2 + 1)[None, :]).reshape(-1)


def local(charge, dest, local_ids, green_hat):
    n_px = lax.axis_size("px")
    n_pz = lax.axis_size("pz")
    n_dev = n_px * n_pz
    wide_x, wide_y = CXP * n_px, CYP * n_pz
    slots = charge.shape[0]
    cap = 2 * slots // n_dev
    pencil_blocks = CXP * CYP * NZP // 128
    own = 2 * wide_y // n_px
    group = 2 * NZP // n_dev

    green = lax.all_to_all(
        green_hat[: wide_x + 1, : own // 2 + 1], "px", split_axis=2, concat_axis=1, tiled=True
    )

    route = dest[:, 0]
    named = (route[:, None] == jnp.arange(n_dev)[None, :]).astype(jnp.bfloat16)
    before = jnp.asarray(np.tril(np.ones((slots, slots)), -1), jnp.bfloat16)
    rank = jnp.sum(
        jnp.einsum("st,td->sd", before, named, preferred_element_type=jnp.float32) * named, axis=1
    ).astype(jnp.int32)
    place = route * cap + rank
    packing = (place[:, None] == jnp.arange(n_dev * cap)[None, :]).astype(jnp.bfloat16)
    sent = pick("sr,sl->rl", packing, charge).reshape(n_dev, cap, 128)
    ids = jnp.einsum(
        "sr,s->r", packing, (local_ids + 1).astype(jnp.bfloat16), preferred_element_type=jnp.float32
    ).reshape(n_dev, 1, cap)
    sent = jnp.concatenate((sent, jnp.pad(ids, ((0, 0), (0, 0), (0, 128 - cap)))), axis=1)
    got = lax.all_to_all(sent, AXES, split_axis=0, concat_axis=0, tiled=True)
    ids = got[:, cap, :cap].reshape(n_dev * cap).astype(jnp.int32) - 1
    placing = (ids[:, None] == jnp.arange(pencil_blocks)[None, :]).astype(jnp.bfloat16)
    field = pick("rb,rl->bl", placing, got[:, :cap].reshape(n_dev * cap, 128))
    field = field.reshape(CXP * CYP, NZP)

    long = split_table(long_table())
    spectrum = product("pz,zk->pk", field, long)
    spectrum = spectrum.reshape(CXP * CYP, n_pz, n_px, group).transpose(2, 1, 0, 3)
    spectrum = spectrum.reshape(n_dev, CXP * CYP, group)
    turned = lax.all_to_all(spectrum, AXES, split_axis=0, concat_axis=0, tiled=True)
    planes = turned.reshape(n_px, n_pz, CXP, CYP, group).transpose(0, 2, 1, 3, 4)
    planes = planes.reshape(wide_x, wide_y, group)

    kept_y = kept_frequencies(wide_y, n_px)
    y_table, y_back = short_tables(wide_y, kept_y)
    x_table, x_back = short_tables(wide_x, np.arange(wide_x + 1))
    planes = product("xyk,qy->xqk", planes, split_table(y_table))
    planes = product("xqk,ux->uqk", planes, split_table(x_table))
    count_x, count_y = wide_x + 1, len(kept_y)
    planes = planes.reshape(2, count_x, 2, count_y, group) * green[None, :, None]
    planes = planes.reshape(2 * count_x, 2 * count_y, group)
    planes = product("uqk,ux->xqk", planes, split_table(x_back))
    planes = product("xqk,qy->xyk", planes, split_table(y_back))

    planes = planes.reshape(n_px, CXP, n_pz, CYP, group).transpose(0, 2, 1, 3, 4)
    planes = planes.reshape(n_dev, CXP * CYP, group)
    turned = lax.all_to_all(planes, AXES, split_axis=0, concat_axis=0, tiled=True)
    spectrum = turned.reshape(n_px, n_pz, CXP * CYP, group).transpose(2, 1, 0, 3)
    spectrum = spectrum.reshape(CXP * CYP, 2 * NZP)
    phi = product("pk,zk->pz", spectrum, long) * (1.0 / (2 * NZP))
    back = pick("rb,bl->rl", placing, phi.reshape(pencil_blocks, 128)).reshape(n_dev, cap, 128)
    got = lax.all_to_all(back, AXES, split_axis=0, concat_axis=0, tiled=True)
    return pick("sr,rl->sl", packing, got.reshape(n_dev * cap, 128))


LANES = 128
GROUP = 64
KEPT = 8
HALF = 32
WIDE = 32
MESH = pl.DeviceIdType.MESH


def unit_rows(frequencies, is_sine, wide):
    period = 2 * wide
    angle = (frequencies[:, None] * np.arange(wide)[None, :] % period) * (2.0 * math.pi / period)
    weight = np.where((frequencies == 0) | (frequencies == wide), 1.0, 2.0) / period
    return np.where(is_sine[:, None], np.sin(angle), np.cos(angle)) * np.sqrt(weight)[:, None]


def plane_tables(n_px, n_pz):
    starts = np.array([0, 16, 33, 49])
    raw = (starts[:, None] + np.arange(KEPT)[None, :]).reshape(-1)
    folded = np.minimum(raw, 2 * WIDE - raw)
    frequencies = np.concatenate((folded, np.where(folded == 0, WIDE, folded)))
    sine = np.concatenate((np.zeros(HALF, bool), folded != 0))
    rows = unit_rows(frequencies, sine, WIDE).reshape(2 * n_px, KEPT, n_pz, CYP)
    eye_i, eye_a = np.eye(n_px), np.eye(4)
    y_table = np.einsum("gqjb,iI,aA->ijabgIqA", rows, eye_i, eye_a)
    y_table = y_table.reshape(n_px * n_pz * 16, 2 * n_px * n_px * KEPT * 4)
    base = np.arange(HALF)
    frequencies = np.concatenate((base, np.where(base == 0, WIDE, base)))
    sine = np.concatenate((np.zeros(HALF, bool), base != 0))
    rows = unit_rows(frequencies, sine, WIDE).reshape(2 * HALF, n_px, 2, 4)
    x_table = np.einsum("uiha,qQ->hiqauQ", rows, np.eye(KEPT))
    x_table = x_table.reshape(2 * n_px * KEPT * 4, 2 * HALF * KEPT)
    return y_table, x_table


def halves(values):
    high = values.astype(jnp.bfloat16)
    return high, (values - high.astype(jnp.float32)).astype(jnp.bfloat16)


def mm(a, b, contract=((1,), (0,))):
    return lax.dot_general(a, b, (contract, ((), ())), preferred_element_type=jnp.float32)


def mm_left(values, high, low, contract=((1,), (0,))):
    v_high, v_low = halves(values)
    rows = values.shape[0]
    both = mm(jnp.concatenate((v_high, v_low), axis=0), high, contract)
    return both[:rows] + (both[rows:] + mm(v_high, low, contract))


def mm_pick(one_hot, values):
    high, low = halves(values)
    return mm(one_hot, high) + mm(one_hot, low)


def iota(shape, axis):
    return lax.broadcasted_iota(jnp.int32, shape, axis)


def as_row(column):
    return jnp.transpose(jnp.broadcast_to(column, (column.shape[0], LANES)))[0:1, :]


def as_column(row):
    return jnp.transpose(jnp.broadcast_to(row, (LANES, row.shape[1])))[:, 0:1]


def one(mask):
    return jnp.where(mask, 1.0, 0.0).astype(jnp.bfloat16)


def fused(
    n_px, n_pz, charge_ref, dest_ref, ids_ref, green_hbm, zh_hbm, zl_hbm, yh_hbm, yl_hbm, xh_hbm,
    xl_hbm, out_ref, green, zh, zl, yh, yl, xh, xl, ids_send, ids_recv, charge_send, charge_recv,
    green_send, green_recv, spec_send, spec_recv, back_send, back_recv, out_send, out_recv, scale,
    load_sems, send_sems, recv_sems
):
    n_dev = n_px * n_pz
    mi, mj = lax.axis_index("px"), lax.axis_index("pz")
    me = mi * n_pz + mj
    slots = charge_ref.shape[0]
    cap = charge_send.shape[1]
    rows = n_dev * cap
    side = n_dev // 2
    near = me // side
    far = 1 - near
    blocks = CXP * CYP * NZP // LANES

    barrier = pltpu.get_barrier_semaphore()

    def greet(step, carry):
        peer = lax.rem(me + step, n_dev)
        pl.semaphore_signal(
            barrier, inc=1, device_id=(peer // n_pz, lax.rem(peer, n_pz)), device_id_type=MESH
        )
        return carry

    lax.fori_loop(1, n_dev, greet, 0)

    loads = [
        pltpu.make_async_copy(source, target, load_sems.at[number])
        for number, (source, target) in enumerate((
            (green_hbm.at[pl.ds(0, 40)], green), (zh_hbm, zh), (zl_hbm, zl), (yh_hbm, yh),
            (yl_hbm, yl), (xh_hbm, xh), (xl_hbm, xl),
        ))
    ]
    for load in loads:
        load.start()

    def block_copy(send, recv, number, peer, part):
        return pltpu.make_async_remote_copy(
            src_ref=send.at[peer],
            dst_ref=recv.at[me],
            send_sem=send_sems.at[number],
            recv_sem=recv_sems.at[number, part],
            device_id=(peer // n_pz, lax.rem(peer, n_pz)),
            device_id_type=MESH,
        )

    def send_far(send, recv, number):
        def body(step, carry):
            block_copy(send, recv, number, far * side + lax.rem(me + step, side), 1).start()
            return carry

        lax.fori_loop(0, side, body, 0)

    def send_near(send, recv, number):
        def body(step, carry):
            block_copy(send, recv, number, near * side + lax.rem(me + step, side), 0).start()
            return carry

        lax.fori_loop(1, side, body, 0)
        recv[me] = send[me]

    def send_all(send, recv, number):
        send_far(send, recv, number)
        send_near(send, recv, number)

    def all_of(send, recv, number, count, part=0):
        return pltpu.make_async_remote_copy(
            src_ref=send.at[pl.ds(0, count)],
            dst_ref=recv.at[pl.ds(0, count)],
            send_sem=send_sems.at[number],
            recv_sem=recv_sems.at[number, part],
            device_id=(mi, mj),
            device_id_type=MESH,
        )

    def wait_near(send, recv, number):
        all_of(send, recv, number, side - 1, 0).wait_recv()

    def wait_far(send, recv, number):
        all_of(send, recv, number, side, 1).wait_recv()

    def wait_both(send, recv, number):
        wait_near(send, recv, number)
        wait_far(send, recv, number)

    dest_row = dest_ref[...].astype(jnp.float32)
    dest = as_column(dest_row)
    named = one(dest == iota((slots, LANES), 1).astype(jnp.float32))
    before = one(iota((slots, slots), 1) < iota((slots, slots), 0))
    rank = jnp.sum(mm(before, named) * named.astype(jnp.float32), axis=1, keepdims=True)
    place = dest * cap + rank
    ids = ids_ref[...].astype(jnp.float32) + 1.0
    owned = jnp.where(dest_row == iota((n_dev, slots), 0).astype(jnp.float32), ids, 0.0)
    ranked = one(rank == iota((slots, LANES), 1).astype(jnp.float32))
    ids_send[...] = mm(owned.astype(jnp.bfloat16), ranked).reshape(n_dev, 1, LANES)
    packing = one(as_row(place) == iota((rows, slots), 0).astype(jnp.float32))
    charge_send[...] = mm_pick(packing, charge_ref[...]).reshape(n_dev, cap, LANES)
    pl.semaphore_wait(barrier, n_dev - 1)
    send_all(ids_send, ids_recv, 0)
    send_all(charge_send, charge_recv, 1)

    loads[0].wait()
    shifted = mi >= n_px // 2
    kept = jnp.where(shifted, green[0:33, 1:9, :], green[0:33, 0:8, :])
    wide = jnp.transpose(kept[0:HALF].reshape(HALF * KEPT, 256))
    edge = green[0:40, 0, :]
    edge = jnp.concatenate((kept[HALF], edge, jnp.zeros((LANES - 48, 256), jnp.float32)), axis=0)
    green_send[...] = jnp.concatenate((wide, jnp.transpose(edge)), axis=1).reshape(n_px, GROUP, 384)

    def green_copy(target):
        return pltpu.make_async_remote_copy(
            src_ref=green_send.at[target],
            dst_ref=green_recv.at[mi],
            send_sem=send_sems.at[2],
            recv_sem=recv_sems.at[2, 0],
            device_id=(target, mj),
            device_id_type=MESH,
        )

    pair_start = near * 2
    for step in range(2):
        green_copy(far * 2 + step).start()
    green_copy(pair_start + 1 - lax.rem(mi, 2)).start()
    green_recv[mi] = green_send[mi]

    wait_both(ids_send, ids_recv, 0)
    line = iota((rows, n_dev), 0)
    spread = mm(one(line // cap == iota((rows, n_dev), 1)), ids_recv[...].reshape(n_dev, LANES).astype(jnp.bfloat16))
    own_lane = iota((rows, LANES), 1) == lax.rem(iota((rows, LANES), 0), cap)
    ids = jnp.sum(jnp.where(own_lane, spread, 0.0), axis=1, keepdims=True)
    lines = CXP * CYP

    def target_of(index):
        return (lax.rem(index, lines) * (NZP // LANES) + index // lines + 1).astype(jnp.float32)

    taking = one(ids == target_of(iota((rows, blocks), 1)))
    placing = one(as_row(ids) == target_of(iota((blocks, rows), 0)))
    wait_both(charge_send, charge_recv, 1)
    field = mm_pick(placing, charge_recv[...].reshape(rows, LANES))
    field = jnp.concatenate([field[lines * c : lines * (c + 1)] for c in range(NZP // LANES)], axis=1)

    f_high, f_low = halves(field)
    f_both = jnp.concatenate((f_high, f_low), axis=0)
    loads[1].wait()
    loads[2].wait()
    first = iota((lines // 2, LANES), 1) < GROUP

    def forward(half, part):
        def body(step, carry):
            two = lax.rem(mj // 2 + step, n_pz // 2)
            columns = pl.ds(pl.multiple_of(half * NZP + two * 256, 256), 256)
            both = mm(f_both, zh[:, columns])
            total = both[:lines] + (both[lines:] + mm(f_high, zl[:, columns]))
            for t in range(2):
                j = two * 2 + t
                tile = total[:, t * LANES : (t + 1) * LANES]
                low, high = tile[: lines // 2], tile[lines // 2 :]
                low_turned, high_turned = pltpu.roll(low, GROUP, 1), pltpu.roll(high, GROUP, 1)
                at = half * side + j
                spec_send[at] = jnp.where(first, low, high_turned)
                spec_send[at + n_pz] = jnp.where(first, low_turned, high)
                for peer in (at, at + n_pz):
                    if part == 1:
                        block_copy(spec_send, spec_recv, 3, peer, 1).start()
                    else:

                        @pl.when(peer != me)
                        def _():
                            block_copy(spec_send, spec_recv, 3, peer, 0).start()

            return carry

        lax.fori_loop(0, n_pz // 2, body, 0)

    forward(far, 1)
    forward(near, 0)
    spec_recv[me] = spec_send[me]

    all_of(green_send, green_recv, 2, n_px - 1).wait_recv()
    lane = iota((GROUP, 256), 1)
    source, target = iota((LANES, 512), 0), iota((LANES, 512), 1)
    wanted = jnp.where(target == 256, HALF, lax.rem(target, 256) // KEPT) + KEPT
    picking = one((source == wanted) & (lax.rem(target, KEPT) == 0))
    e_high, e_low = halves(green_recv[2, :, 256:384])
    e_rest = (green_recv[2, :, 256:384] - e_high.astype(jnp.float32) - e_low.astype(jnp.float32)).astype(jnp.bfloat16)
    nyquist = mm(e_high, picking) + (mm(e_low, picking) + mm(e_rest, picking))
    for i in range(n_px):
        wide = green_recv[i, :, 0:256]
        edge = jnp.concatenate((green_recv[i, :, 256:384], wide[:, LANES:]), axis=1)
        full = jnp.concatenate((wide, jnp.where(lane < KEPT, edge, wide)), axis=1)
        scale[i * GROUP : (i + 1) * GROUP, :] = full
        if i == 0:
            full = jnp.where(lax.rem(iota((GROUP, 512), 1), KEPT) == 0, nyquist, full)
        scale[(n_px + i) * GROUP : (n_px + i + 1) * GROUP, :] = full

    for load in loads[3:]:
        load.wait()

    def side_planes(half):
        taken = spec_recv[pl.ds(half * side, side)].reshape(side * 16, LANES)
        table_rows = pl.ds(pl.multiple_of(half * (side * 16), side * 16), side * 16)
        return mm_left(jnp.transpose(taken), yh[table_rows, :], yl[table_rows, :])

    wait_near(spec_send, spec_recv, 3)
    planes = side_planes(near)
    wait_far(spec_send, spec_recv, 3)
    planes = planes + side_planes(far)
    groups = 2 * n_px
    planes = jnp.concatenate(
        [
            jnp.concatenate(
                [planes[h * GROUP : (h + 1) * GROUP, g * LANES : (g + 1) * LANES] for h in range(2)], axis=1
            )
            for g in range(groups)
        ],
        axis=0,
    )
    planes = mm_left(planes, xh[...], xl[...]) * scale[...]
    planes = mm_left(planes, xh[...], xl[...], ((1,), (1,)))
    planes = jnp.concatenate(
        [
            jnp.concatenate(
                [planes[g * GROUP : (g + 1) * GROUP, h * LANES : (h + 1) * LANES] for g in range(groups)], axis=1
            )
            for h in range(2)
        ],
        axis=0,
    )
    p_high, p_low = halves(planes)
    right = ((1,), (1,))

    def side_back(half):
        table_rows = pl.ds(pl.multiple_of(half * (side * 16), side * 16), side * 16)
        high, low = yh[table_rows, :], yl[table_rows, :]
        given = mm(high, p_high, right) + (mm(high, p_low, right) + mm(low, p_high, right))
        back_send[pl.ds(half * side, side)] = given.reshape(side, 16, LANES)

    side_back(far)
    send_far(back_send, back_recv, 4)
    side_back(near)
    send_near(back_send, back_recv, 4)

    def side_phi(half):
        pieces = []
        for j in range(n_pz):
            left, other = back_recv[half * side + j], back_recv[half * side + n_pz + j]
            low = jnp.where(first, left, pltpu.roll(other, GROUP, 1))
            high = jnp.where(first, pltpu.roll(left, GROUP, 1), other)
            pieces.append(jnp.concatenate((low, high), axis=0))
        columns = pl.ds(pl.multiple_of(half * NZP, NZP), NZP)
        return mm_left(jnp.concatenate(pieces, axis=1), zh[:, columns], zl[:, columns], right)

    wait_near(back_send, back_recv, 4)
    phi = side_phi(near)
    wait_far(back_send, back_recv, 4)
    phi = phi + side_phi(far)
    phi = jnp.concatenate([phi[:, c * LANES : (c + 1) * LANES] for c in range(NZP // LANES)], axis=0)
    out_send[...] = mm_pick(taking, phi).reshape(n_dev, cap, LANES)
    send_all(out_send, out_recv, 5)
    unpacking = one(place == iota((slots, rows), 1).astype(jnp.float32))
    wait_both(out_send, out_recv, 5)
    out_ref[...] = mm_pick(unpacking, out_recv[...].reshape(rows, LANES))

    all_of(ids_send, ids_recv, 0, n_dev - 1).wait_send()
    all_of(charge_send, charge_recv, 1, n_dev - 1).wait_send()
    all_of(green_send, green_recv, 2, n_px - 1).wait_send()
    all_of(spec_send, spec_recv, 3, n_dev - 1).wait_send()
    all_of(back_send, back_recv, 4, n_dev - 1).wait_send()
    all_of(out_send, out_recv, 5, n_dev - 1).wait_send()


def local_fused(charge, dest, local_ids, green_hat):
    n_px, n_pz = lax.axis_size("px"), lax.axis_size("pz")
    n_dev = n_px * n_pz
    slots = charge.shape[0]
    cap = 2 * slots // n_dev
    y_table, x_table = plane_tables(n_px, n_pz)
    z_table = long_table().reshape(NZP, n_pz, 2, 2 * GROUP).transpose(0, 2, 1, 3)
    z_table = z_table.reshape(NZP, 2 * NZP) / math.sqrt(2 * NZP)
    tables = [
        piece
        for table in (z_table, y_table, x_table)
        for piece in split_table(table)
    ]
    exchange = lambda lead, rows: [pltpu.VMEM((lead, rows, LANES), jnp.float32)] * 2
    vmem, anywhere = pl.BlockSpec(memory_space=pltpu.VMEM), pl.BlockSpec(memory_space=pltpu.HBM)
    return pl.pallas_call(
        functools.partial(fused, n_px, n_pz),
        out_shape=jax.ShapeDtypeStruct(charge.shape, jnp.float32),
        in_specs=[vmem] * 3 + [anywhere] * 7,
        out_specs=vmem,
        scratch_shapes=[
            pltpu.VMEM((40,) + green_hat.shape[1:], jnp.float32),
            *[pltpu.VMEM(table.shape, jnp.bfloat16) for table in tables],
            *exchange(n_dev, 1),
            *exchange(n_dev, cap),
            *[pltpu.VMEM((n_px, GROUP, 384), jnp.float32)] * 2,
            *exchange(n_dev, 16),
            *exchange(n_dev, 16),
            *exchange(n_dev, cap),
            pltpu.VMEM((2 * n_px * GROUP, 2 * HALF * KEPT), jnp.float32),
            pltpu.SemaphoreType.DMA((7,)),
            pltpu.SemaphoreType.DMA((6,)),
            pltpu.SemaphoreType.DMA((6, 2)),
        ],
        compiler_params=pltpu.CompilerParams(
            collective_id=0, has_side_effects=True, vmem_limit_bytes=48 * 1024 * 1024
        ),
    )(charge, dest.reshape(1, slots), local_ids.reshape(1, slots), green_hat, *tables)


def solution(mesh):
    planes = mesh.shape["px"] == 4 and mesh.shape["pz"] == 8
    return jax.shard_map(
        local_fused if planes else local,
        mesh=mesh,
        in_specs=(
            P(AXES, None),
            P(AXES, None),
            P(AXES),
            P(None, "px", "pz"),
        ),
        out_specs=P(AXES, None),
        check_vma=False,
    )
```

```python
import functools
import math

import jax
import jax.numpy as jnp
import numpy as np
from jax import lax
from jax.experimental import pallas as pl
from jax.experimental.pallas import tpu as pltpu
from jax.sharding import PartitionSpec as P

CXP = 8
CYP = 4
NZP = 1024
AXES = ("px", "pz")


def split_table(table):
    high = table.astype(np.float32).astype(jnp.bfloat16)
    low = (table - high.astype(np.float64)).astype(np.float32).astype(jnp.bfloat16)
    return np.asarray(high), np.asarray(low)


def long_table():
    n = np.arange(NZP)[:, None]
    k = np.arange(2 * NZP)[None, :]
    angle = (n * k % (2 * NZP)) * (2.0 * math.pi / (2 * NZP))
    return np.cos(angle) + np.sin(angle)


def short_tables(wide, frequencies):
    period = 2 * wide
    folded = np.minimum(frequencies, period - frequencies)
    angle = (frequencies[:, None] * np.arange(wide)[None, :] % period) * (2.0 * math.pi / period)
    table = np.concatenate((np.cos(angle), np.sin(angle)), axis=0)
    weight = np.where((folded == 0) | (folded == wide), 1.0, 2.0) / period
    count = np.array([(folded == f).sum() for f in folded])
    weight = np.tile(weight / count, 2)
    return table, table * weight[:, None]


def split(values):
    high = lax.reduce_precision(values, 8, 7)
    return high.astype(jnp.bfloat16), (values - high).astype(jnp.bfloat16)


def product(form, values, table):
    high, low = split(values)
    t_high, t_low = table
    dot = lambda a, b: jnp.einsum(form, a, b, preferred_element_type=jnp.float32)
    return dot(high, t_high) + (dot(low, t_high) + dot(high, t_low))


def pick(form, one_hot, values):
    high, low = split(values)
    dot = lambda b: jnp.einsum(form, one_hot, b, preferred_element_type=jnp.float32)
    return dot(high) + dot(low)


def kept_frequencies(wide_y, n_px):
    own = 2 * wide_y // n_px
    return (np.arange(n_px)[:, None] * own + np.arange(own // 2 + 1)[None, :]).reshape(-1)


def local(charge, dest, local_ids, green_hat):
    n_px = lax.axis_size("px")
    n_pz = lax.axis_size("pz")
    n_dev = n_px * n_pz
    wide_x, wide_y = CXP * n_px, CYP * n_pz
    slots = charge.shape[0]
    cap = 2 * slots // n_dev
    pencil_blocks = CXP * CYP * NZP // 128
    own = 2 * wide_y // n_px
    group = 2 * NZP // n_dev

    green = lax.all_to_all(
        green_hat[: wide_x + 1, : own // 2 + 1], "px", split_axis=2, concat_axis=1, tiled=True
    )

    route = dest[:, 0]
    named = (route[:, None] == jnp.arange(n_dev)[None, :]).astype(jnp.bfloat16)
    before = jnp.asarray(np.tril(np.ones((slots, slots)), -1), jnp.bfloat16)
    rank = jnp.sum(
        jnp.einsum("st,td->sd", before, named, preferred_element_type=jnp.float32) * named, axis=1
    ).astype(jnp.int32)
    place = route * cap + rank
    packing = (place[:, None] == jnp.arange(n_dev * cap)[None, :]).astype(jnp.bfloat16)
    sent = pick("sr,sl->rl", packing, charge).reshape(n_dev, cap, 128)
    ids = jnp.einsum(
        "sr,s->r", packing, (local_ids + 1).astype(jnp.bfloat16), preferred_element_type=jnp.float32
    ).reshape(n_dev, 1, cap)
    sent = jnp.concatenate((sent, jnp.pad(ids, ((0, 0), (0, 0), (0, 128 - cap)))), axis=1)
    got = lax.all_to_all(sent, AXES, split_axis=0, concat_axis=0, tiled=True)
    ids = got[:, cap, :cap].reshape(n_dev * cap).astype(jnp.int32) - 1
    placing = (ids[:, None] == jnp.arange(pencil_blocks)[None, :]).astype(jnp.bfloat16)
    field = pick("rb,rl->bl", placing, got[:, :cap].reshape(n_dev * cap, 128))
    field = field.reshape(CXP * CYP, NZP)

    long = split_table(long_table())
    spectrum = product("pz,zk->pk", field, long)
    spectrum = spectrum.reshape(CXP * CYP, n_pz, n_px, group).transpose(2, 1, 0, 3)
    spectrum = spectrum.reshape(n_dev, CXP * CYP, group)
    turned = lax.all_to_all(spectrum, AXES, split_axis=0, concat_axis=0, tiled=True)
    planes = turned.reshape(n_px, n_pz, CXP, CYP, group).transpose(0, 2, 1, 3, 4)
    planes = planes.reshape(wide_x, wide_y, group)

    kept_y = kept_frequencies(wide_y, n_px)
    y_table, y_back = short_tables(wide_y, kept_y)
    x_table, x_back = short_tables(wide_x, np.arange(wide_x + 1))
    planes = product("xyk,qy->xqk", planes, split_table(y_table))
    planes = product("xqk,ux->uqk", planes, split_table(x_table))
    count_x, count_y = wide_x + 1, len(kept_y)
    planes = planes.reshape(2, count_x, 2, count_y, group) * green[None, :, None]
    planes = planes.reshape(2 * count_x, 2 * count_y, group)
    planes = product("uqk,ux->xqk", planes, split_table(x_back))
    planes = product("xqk,qy->xyk", planes, split_table(y_back))

    planes = planes.reshape(n_px, CXP, n_pz, CYP, group).transpose(0, 2, 1, 3, 4)
    planes = planes.reshape(n_dev, CXP * CYP, group)
    turned = lax.all_to_all(planes, AXES, split_axis=0, concat_axis=0, tiled=True)
    spectrum = turned.reshape(n_px, n_pz, CXP * CYP, group).transpose(2, 1, 0, 3)
    spectrum = spectrum.reshape(CXP * CYP, 2 * NZP)
    phi = product("pk,zk->pz", spectrum, long) * (1.0 / (2 * NZP))
    back = pick("rb,bl->rl", placing, phi.reshape(pencil_blocks, 128)).reshape(n_dev, cap, 128)
    got = lax.all_to_all(back, AXES, split_axis=0, concat_axis=0, tiled=True)
    return pick("sr,rl->sl", packing, got.reshape(n_dev * cap, 128))


LANES = 128
GROUP = 64
KEPT = 8
HALF = 32
WIDE = 32
MESH = pl.DeviceIdType.MESH


def unit_rows(frequencies, is_sine, wide):
    period = 2 * wide
    angle = (frequencies[:, None] * np.arange(wide)[None, :] % period) * (2.0 * math.pi / period)
    weight = np.where((frequencies == 0) | (frequencies == wide), 1.0, 2.0) / period
    return np.where(is_sine[:, None], np.sin(angle), np.cos(angle)) * np.sqrt(weight)[:, None]


def plane_tables(n_px, n_pz):
    y_tables = []
    for half in range(2):
        raw = half * WIDE + np.arange(HALF)
        folded = np.minimum(raw, 2 * WIDE - raw)
        lone = folded == folded[0]
        frequencies = np.concatenate((folded, np.where(lone, WIDE - folded[0], folded)))
        sine = np.concatenate((np.zeros(HALF, bool), ~lone))
        rows = unit_rows(frequencies, sine, WIDE).reshape(2 * n_px, KEPT, n_pz, CYP)
        table = np.einsum("gqjb,iI,aA->ijabgIqA", rows, np.eye(n_px), np.eye(4))
        y_tables.append(table.reshape(n_px * n_pz * 16, 2 * n_px * n_px * KEPT * 4))
    y_table = np.stack(y_tables)
    base = np.arange(HALF)
    frequencies = np.concatenate((base, np.where(base == 0, WIDE, base)))
    sine = np.concatenate((np.zeros(HALF, bool), base != 0))
    rows = unit_rows(frequencies, sine, WIDE).reshape(2 * HALF, n_px, 2, 4)
    x_table = np.einsum("uiha,qQ->hiqauQ", rows, np.eye(KEPT))
    x_table = x_table.reshape(2 * n_px * KEPT * 4, 2 * HALF * KEPT)
    return y_table, x_table


def halves(values):
    high = values.astype(jnp.bfloat16)
    return high, (values - high.astype(jnp.float32)).astype(jnp.bfloat16)


def mm(a, b, contract=((1,), (0,))):
    return lax.dot_general(a, b, (contract, ((), ())), preferred_element_type=jnp.float32)


def mm_left(values, high, low, contract=((1,), (0,))):
    v_high, v_low = halves(values)
    rows = values.shape[0]
    both = mm(jnp.concatenate((v_high, v_low), axis=0), high, contract)
    return both[:rows] + (both[rows:] + mm(v_high, low, contract))


def mm_pick(one_hot, values):
    high, low = halves(values)
    return mm(one_hot, high) + mm(one_hot, low)


def iota(shape, axis):
    return lax.broadcasted_iota(jnp.int32, shape, axis)


def as_row(column):
    return jnp.transpose(jnp.broadcast_to(column, (column.shape[0], LANES)))[0:1, :]


def as_column(row):
    return jnp.transpose(jnp.broadcast_to(row, (LANES, row.shape[1])))[:, 0:1]


def one(mask):
    return jnp.where(mask, 1.0, 0.0).astype(jnp.bfloat16)


def fused(
    n_px, n_pz, charge_ref, dest_ref, ids_ref, green_hbm, zh_hbm, zl_hbm, yh_hbm, yl_hbm, xh_hbm,
    xl_hbm, out_ref, green, zh, zl, yh, yl, xh, xl, ids_send, ids_recv, charge_send, charge_recv,
    green_send, green_recv, edge_recv, spec_send, spec_recv, back_send, back_recv, out_send, out_recv, scale,
    load_sems, green_sems, send_sems, recv_sems
):
    n_dev = n_px * n_pz
    mi, mj = lax.axis_index("px"), lax.axis_index("pz")
    me = mi * n_pz + mj
    slots = charge_ref.shape[0]
    cap = charge_send.shape[1]
    rows = n_dev * cap
    side = n_dev // 2
    near = me // side
    far = 1 - near
    blocks = CXP * CYP * NZP // LANES

    barrier = pltpu.get_barrier_semaphore()

    def greet(step, carry):
        peer = lax.rem(me + step, n_dev)
        pl.semaphore_signal(
            barrier, inc=1, device_id=(peer // n_pz, lax.rem(peer, n_pz)), device_id_type=MESH
        )
        return carry

    lax.fori_loop(1, n_dev, greet, 0)

    loads = [
        pltpu.make_async_copy(source, target, load_sems.at[number])
        for number, (source, target) in enumerate((
            (green_hbm.at[pl.ds(0, 40)], green), (zh_hbm, zh), (zl_hbm, zl), (yh_hbm.at[near], yh),
            (yl_hbm.at[near], yl), (xh_hbm, xh), (xl_hbm, xl),
        ))
    ]
    for load in loads:
        load.start()

    def block_copy(send, recv, number, peer, part):
        return pltpu.make_async_remote_copy(
            src_ref=send.at[peer],
            dst_ref=recv.at[me],
            send_sem=send_sems.at[number],
            recv_sem=recv_sems.at[number, part],
            device_id=(peer // n_pz, lax.rem(peer, n_pz)),
            device_id_type=MESH,
        )

    def send_far(send, recv, number):
        def body(step, carry):
            block_copy(send, recv, number, far * side + lax.rem(me + step, side), 1).start()
            return carry

        lax.fori_loop(0, side, body, 0)

    def send_near(send, recv, number):
        def body(step, carry):
            block_copy(send, recv, number, near * side + lax.rem(me + step, side), 0).start()
            return carry

        lax.fori_loop(1, side, body, 0)
        recv[me] = send[me]

    def send_all(send, recv, number):
        send_far(send, recv, number)
        send_near(send, recv, number)

    def all_of(send, recv, number, count, part=0):
        return pltpu.make_async_remote_copy(
            src_ref=send.at[pl.ds(0, count)],
            dst_ref=recv.at[pl.ds(0, count)],
            send_sem=send_sems.at[number],
            recv_sem=recv_sems.at[number, part],
            device_id=(mi, mj),
            device_id_type=MESH,
        )

    def wait_near(send, recv, number):
        all_of(send, recv, number, side - 1, 0).wait_recv()

    def wait_far(send, recv, number):
        all_of(send, recv, number, side, 1).wait_recv()

    def wait_both(send, recv, number):
        wait_near(send, recv, number)
        wait_far(send, recv, number)

    dest_row = dest_ref[...].astype(jnp.float32)
    dest = as_column(dest_row)
    named = one(dest == iota((slots, LANES), 1).astype(jnp.float32))
    before = one(iota((slots, slots), 1) < iota((slots, slots), 0))
    rank = jnp.sum(mm(before, named) * named.astype(jnp.float32), axis=1, keepdims=True)
    place = dest * cap + rank
    ids = ids_ref[...].astype(jnp.float32) + 1.0
    owned = jnp.where(dest_row == iota((n_dev, slots), 0).astype(jnp.float32), ids, 0.0)
    ranked = one(rank == iota((slots, LANES), 1).astype(jnp.float32))
    ids_send[...] = mm(owned.astype(jnp.bfloat16), ranked).reshape(n_dev, 1, LANES)
    packing = one(as_row(place) == iota((rows, slots), 0).astype(jnp.float32))
    charge_send[...] = mm_pick(packing, charge_ref[...]).reshape(n_dev, cap, LANES)
    pl.semaphore_wait(barrier, n_dev - 1)
    send_all(ids_send, ids_recv, 0)
    send_all(charge_send, charge_recv, 1)

    loads[0].wait()
    wide = [jnp.transpose(green[0:HALF, t * KEPT : (t + 1) * KEPT, :].reshape(HALF * KEPT, 256)) for t in range(2)]
    edge = jnp.concatenate((green[HALF], green[0:40, 0, :], jnp.zeros((LANES - 56, 256), jnp.float32)), axis=0)
    green_send[...] = jnp.concatenate((*wide, jnp.transpose(edge)), axis=1).reshape(n_px, GROUP, 640)
    odd = lax.rem(mi, 2)
    partner = mi + 1 - 2 * odd
    green_copy = pltpu.make_async_remote_copy(
        src_ref=green_send.at[partner],
        dst_ref=green_recv.at[odd],
        send_sem=green_sems.at[0],
        recv_sem=green_sems.at[3],
        device_id=(partner, mj),
        device_id_type=MESH,
    )
    green_copy.start()

    def edge_copy(step):
        target = far * 2 + step
        return pltpu.make_async_remote_copy(
            src_ref=green_send.at[target, :, pl.ds(512, LANES)],
            dst_ref=edge_recv,
            send_sem=green_sems.at[1 + step],
            recv_sem=green_sems.at[4],
            device_id=(target, mj),
            device_id_type=MESH,
        )

    @pl.when(odd == 0)
    def _():
        for step in range(2):
            edge_copy(step).start()

    green_recv[odd] = green_send[mi]

    wait_both(ids_send, ids_recv, 0)
    line = iota((rows, n_dev), 0)
    spread = mm(one(line // cap == iota((rows, n_dev), 1)), ids_recv[...].reshape(n_dev, LANES).astype(jnp.bfloat16))
    own_lane = iota((rows, LANES), 1) == lax.rem(iota((rows, LANES), 0), cap)
    ids = jnp.sum(jnp.where(own_lane, spread, 0.0), axis=1, keepdims=True)
    lines = CXP * CYP

    def target_of(index):
        return (lax.rem(index, lines) * (NZP // LANES) + index // lines + 1).astype(jnp.float32)

    taking = one(ids == target_of(iota((rows, blocks), 1)))
    placing = one(as_row(ids) == target_of(iota((blocks, rows), 0)))
    wait_both(charge_send, charge_recv, 1)
    field = mm_pick(placing, charge_recv[...].reshape(rows, LANES))
    field = jnp.concatenate([field[lines * c : lines * (c + 1)] for c in range(NZP // LANES)], axis=1)

    f_high, f_low = halves(field)
    f_both = jnp.concatenate((f_high, f_low), axis=0)
    loads[1].wait()
    loads[2].wait()
    first = iota((lines // 2, LANES), 1) < GROUP

    def forward(half, part):
        def body(step, carry):
            two = lax.rem(mj // 2 + step, n_pz // 2)
            columns = pl.ds(pl.multiple_of(half * NZP + two * 256, 256), 256)
            both = mm(f_both, zh[:, columns])
            total = both[:lines] + (both[lines:] + mm(f_high, zl[:, columns]))
            for t in range(2):
                j = two * 2 + t
                tile = total[:, t * LANES : (t + 1) * LANES]
                low, high = tile[: lines // 2], tile[lines // 2 :]
                low_turned, high_turned = pltpu.roll(low, GROUP, 1), pltpu.roll(high, GROUP, 1)
                at = half * side + j
                spec_send[at] = jnp.where(first, low, high_turned)
                spec_send[at + n_pz] = jnp.where(first, low_turned, high)
                for peer in (at, at + n_pz):
                    if part == 1:
                        block_copy(spec_send, spec_recv, 3, peer, 1).start()
                    else:

                        @pl.when(peer != me)
                        def _():
                            block_copy(spec_send, spec_recv, 3, peer, 0).start()

            return carry

        lax.fori_loop(0, n_pz // 2, body, 0)

    forward(far, 1)
    forward(near, 0)
    spec_recv[me] = spec_send[me]

    green_copy.wait_recv()
    edge_copy(0).wait_recv()
    source, target = iota((LANES, 512), 0), iota((LANES, 512), 1)
    wanted = jnp.where(target == 256, HALF, lax.rem(target, 256) // KEPT) + 2 * KEPT
    picking = one((source == wanted) & (lax.rem(target, KEPT) == 0))
    e_high, e_low = halves(edge_recv[...])
    lone = mm(e_high, picking) + mm(e_low, picking)
    lane = iota((GROUP, LANES), 1)
    for parity in range(2):
        edge = green_recv[parity, :, 512:640]
        for t in range(2):
            wide = green_recv[parity, :, t * 256 : (t + 1) * 256]
            turned = edge if t == 0 else pltpu.roll(edge, LANES - KEPT, 1)
            start = jnp.where(lane < KEPT, turned, wide[:, :LANES])
            full = jnp.concatenate((wide, start, wide[:, LANES:]), axis=1)
            at = (2 * parity + t) * GROUP
            scale[at : at + GROUP, :] = full
            if parity == 0 and t == 0:
                full = jnp.where(lax.rem(iota((GROUP, 512), 1), KEPT) == 0, lone, full)
            at = at + n_px * GROUP
            scale[at : at + GROUP, :] = full

    for load in loads[3:]:
        load.wait()

    def side_planes(half):
        taken = spec_recv[pl.ds(half * side, side)].reshape(side * 16, LANES)
        table_rows = pl.ds(pl.multiple_of(half * (side * 16), side * 16), side * 16)
        return mm_left(jnp.transpose(taken), yh[table_rows, :], yl[table_rows, :])

    wait_near(spec_send, spec_recv, 3)
    planes = side_planes(near)
    wait_far(spec_send, spec_recv, 3)
    planes = planes + side_planes(far)
    groups = 2 * n_px
    planes = jnp.concatenate(
        [
            jnp.concatenate(
                [planes[h * GROUP : (h + 1) * GROUP, g * LANES : (g + 1) * LANES] for h in range(2)], axis=1
            )
            for g in range(groups)
        ],
        axis=0,
    )
    planes = mm_left(planes, xh[...], xl[...]) * scale[...]
    planes = mm_left(planes, xh[...], xl[...], ((1,), (1,)))
    planes = jnp.concatenate(
        [
            jnp.concatenate(
                [planes[g * GROUP : (g + 1) * GROUP, h * LANES : (h + 1) * LANES] for g in range(groups)], axis=1
            )
            for h in range(2)
        ],
        axis=0,
    )
    p_high, p_low = halves(planes)
    right = ((1,), (1,))

    def side_back(half):
        table_rows = pl.ds(pl.multiple_of(half * (side * 16), side * 16), side * 16)
        high, low = yh[table_rows, :], yl[table_rows, :]
        given = mm(high, p_high, right) + (mm(high, p_low, right) + mm(low, p_high, right))
        back_send[pl.ds(half * side, side)] = given.reshape(side, 16, LANES)

    side_back(far)
    send_far(back_send, back_recv, 4)
    side_back(near)
    send_near(back_send, back_recv, 4)

    def side_phi(half):
        pieces = []
        for j in range(n_pz):
            left, other = back_recv[half * side + j], back_recv[half * side + n_pz + j]
            low = jnp.where(first, left, pltpu.roll(other, GROUP, 1))
            high = jnp.where(first, pltpu.roll(left, GROUP, 1), other)
            pieces.append(jnp.concatenate((low, high), axis=0))
        columns = pl.ds(pl.multiple_of(half * NZP, NZP), NZP)
        return mm_left(jnp.concatenate(pieces, axis=1), zh[:, columns], zl[:, columns], right)

    wait_near(back_send, back_recv, 4)
    phi = side_phi(near)
    wait_far(back_send, back_recv, 4)
    phi = phi + side_phi(far)
    phi = jnp.concatenate([phi[:, c * LANES : (c + 1) * LANES] for c in range(NZP // LANES)], axis=0)
    out_send[...] = mm_pick(taking, phi).reshape(n_dev, cap, LANES)
    send_all(out_send, out_recv, 5)
    unpacking = one(place == iota((slots, rows), 1).astype(jnp.float32))
    wait_both(out_send, out_recv, 5)
    out_ref[...] = mm_pick(unpacking, out_recv[...].reshape(rows, LANES))

    all_of(ids_send, ids_recv, 0, n_dev - 1).wait_send()
    all_of(charge_send, charge_recv, 1, n_dev - 1).wait_send()
    green_copy.wait_send()

    @pl.when(odd == 0)
    def _():
        for step in range(2):
            edge_copy(step).wait_send()

    all_of(spec_send, spec_recv, 3, n_dev - 1).wait_send()
    all_of(back_send, back_recv, 4, n_dev - 1).wait_send()
    all_of(out_send, out_recv, 5, n_dev - 1).wait_send()


def local_fused(charge, dest, local_ids, green_hat):
    n_px, n_pz = lax.axis_size("px"), lax.axis_size("pz")
    n_dev = n_px * n_pz
    slots = charge.shape[0]
    cap = 2 * slots // n_dev
    y_table, x_table = plane_tables(n_px, n_pz)
    z_table = long_table().reshape(NZP, n_pz, 2, 2 * GROUP).transpose(0, 2, 1, 3)
    z_table = z_table.reshape(NZP, 2 * NZP) / math.sqrt(2 * NZP)
    tables = [
        piece
        for table in (z_table, y_table, x_table)
        for piece in split_table(table)
    ]
    exchange = lambda lead, rows: [pltpu.VMEM((lead, rows, LANES), jnp.float32)] * 2
    vmem, anywhere = pl.BlockSpec(memory_space=pltpu.VMEM), pl.BlockSpec(memory_space=pltpu.HBM)
    return pl.pallas_call(
        functools.partial(fused, n_px, n_pz),
        out_shape=jax.ShapeDtypeStruct(charge.shape, jnp.float32),
        in_specs=[vmem] * 3 + [anywhere] * 7,
        out_specs=vmem,
        scratch_shapes=[
            pltpu.VMEM((40,) + green_hat.shape[1:], jnp.float32),
            *[pltpu.VMEM(table.shape[-2:], jnp.bfloat16) for table in tables],
            *exchange(n_dev, 1),
            *exchange(n_dev, cap),
            pltpu.VMEM((n_px, GROUP, 640), jnp.float32),
            pltpu.VMEM((2, GROUP, 640), jnp.float32),
            pltpu.VMEM((GROUP, LANES), jnp.float32),
            *exchange(n_dev, 16),
            *exchange(n_dev, 16),
            *exchange(n_dev, cap),
            pltpu.VMEM((2 * n_px * GROUP, 2 * HALF * KEPT), jnp.float32),
            pltpu.SemaphoreType.DMA((7,)),
            pltpu.SemaphoreType.DMA((5,)),
            pltpu.SemaphoreType.DMA((6,)),
            pltpu.SemaphoreType.DMA((6, 2)),
        ],
        compiler_params=pltpu.CompilerParams(
            collective_id=0, has_side_effects=True, vmem_limit_bytes=64 * 1024 * 1024
        ),
    )(charge, dest.reshape(1, slots), local_ids.reshape(1, slots), green_hat, *tables)


def solution(mesh):
    planes = mesh.shape["px"] == 4 and mesh.shape["pz"] == 8
    return jax.shard_map(
        local_fused if planes else local,
        mesh=mesh,
        in_specs=(
            P(AXES, None),
            P(AXES, None),
            P(AXES),
            P(None, "px", "pz"),
        ),
        out_specs=P(AXES, None),
        check_vma=False,
    )
```

```python
import functools
import math

import jax
import jax.numpy as jnp
import numpy as np
from jax import lax
from jax.experimental import pallas as pl
from jax.experimental.pallas import tpu as pltpu
from jax.sharding import PartitionSpec as P

CXP = 8
CYP = 4
NZP = 1024
AXES = ("px", "pz")


def split_table(table):
    high = table.astype(np.float32).astype(jnp.bfloat16)
    low = (table - high.astype(np.float64)).astype(np.float32).astype(jnp.bfloat16)
    return np.asarray(high), np.asarray(low)


def long_table():
    n = np.arange(NZP)[:, None]
    k = np.arange(2 * NZP)[None, :]
    angle = (n * k % (2 * NZP)) * (2.0 * math.pi / (2 * NZP))
    return np.cos(angle) + np.sin(angle)


def short_tables(wide, frequencies):
    period = 2 * wide
    folded = np.minimum(frequencies, period - frequencies)
    angle = (frequencies[:, None] * np.arange(wide)[None, :] % period) * (2.0 * math.pi / period)
    table = np.concatenate((np.cos(angle), np.sin(angle)), axis=0)
    weight = np.where((folded == 0) | (folded == wide), 1.0, 2.0) / period
    count = np.array([(folded == f).sum() for f in folded])
    weight = np.tile(weight / count, 2)
    return table, table * weight[:, None]


def split(values):
    high = lax.reduce_precision(values, 8, 7)
    return high.astype(jnp.bfloat16), (values - high).astype(jnp.bfloat16)


def product(form, values, table):
    high, low = split(values)
    t_high, t_low = table
    dot = lambda a, b: jnp.einsum(form, a, b, preferred_element_type=jnp.float32)
    return dot(high, t_high) + (dot(low, t_high) + dot(high, t_low))


def pick(form, one_hot, values):
    high, low = split(values)
    dot = lambda b: jnp.einsum(form, one_hot, b, preferred_element_type=jnp.float32)
    return dot(high) + dot(low)


def kept_frequencies(wide_y, n_px):
    own = 2 * wide_y // n_px
    return (np.arange(n_px)[:, None] * own + np.arange(own // 2 + 1)[None, :]).reshape(-1)


def local(charge, dest, local_ids, green_hat):
    n_px = lax.axis_size("px")
    n_pz = lax.axis_size("pz")
    n_dev = n_px * n_pz
    wide_x, wide_y = CXP * n_px, CYP * n_pz
    slots = charge.shape[0]
    cap = 2 * slots // n_dev
    pencil_blocks = CXP * CYP * NZP // 128
    own = 2 * wide_y // n_px
    group = 2 * NZP // n_dev

    green = lax.all_to_all(
        green_hat[: wide_x + 1, : own // 2 + 1], "px", split_axis=2, concat_axis=1, tiled=True
    )

    route = dest[:, 0]
    named = (route[:, None] == jnp.arange(n_dev)[None, :]).astype(jnp.bfloat16)
    before = jnp.asarray(np.tril(np.ones((slots, slots)), -1), jnp.bfloat16)
    rank = jnp.sum(
        jnp.einsum("st,td->sd", before, named, preferred_element_type=jnp.float32) * named, axis=1
    ).astype(jnp.int32)
    place = route * cap + rank
    packing = (place[:, None] == jnp.arange(n_dev * cap)[None, :]).astype(jnp.bfloat16)
    sent = pick("sr,sl->rl", packing, charge).reshape(n_dev, cap, 128)
    ids = jnp.einsum(
        "sr,s->r", packing, (local_ids + 1).astype(jnp.bfloat16), preferred_element_type=jnp.float32
    ).reshape(n_dev, 1, cap)
    sent = jnp.concatenate((sent, jnp.pad(ids, ((0, 0), (0, 0), (0, 128 - cap)))), axis=1)
    got = lax.all_to_all(sent, AXES, split_axis=0, concat_axis=0, tiled=True)
    ids = got[:, cap, :cap].reshape(n_dev * cap).astype(jnp.int32) - 1
    placing = (ids[:, None] == jnp.arange(pencil_blocks)[None, :]).astype(jnp.bfloat16)
    field = pick("rb,rl->bl", placing, got[:, :cap].reshape(n_dev * cap, 128))
    field = field.reshape(CXP * CYP, NZP)

    long = split_table(long_table())
    spectrum = product("pz,zk->pk", field, long)
    spectrum = spectrum.reshape(CXP * CYP, n_pz, n_px, group).transpose(2, 1, 0, 3)
    spectrum = spectrum.reshape(n_dev, CXP * CYP, group)
    turned = lax.all_to_all(spectrum, AXES, split_axis=0, concat_axis=0, tiled=True)
    planes = turned.reshape(n_px, n_pz, CXP, CYP, group).transpose(0, 2, 1, 3, 4)
    planes = planes.reshape(wide_x, wide_y, group)

    kept_y = kept_frequencies(wide_y, n_px)
    y_table, y_back = short_tables(wide_y, kept_y)
    x_table, x_back = short_tables(wide_x, np.arange(wide_x + 1))
    planes = product("xyk,qy->xqk", planes, split_table(y_table))
    planes = product("xqk,ux->uqk", planes, split_table(x_table))
    count_x, count_y = wide_x + 1, len(kept_y)
    planes = planes.reshape(2, count_x, 2, count_y, group) * green[None, :, None]
    planes = planes.reshape(2 * count_x, 2 * count_y, group)
    planes = product("uqk,ux->xqk", planes, split_table(x_back))
    planes = product("xqk,qy->xyk", planes, split_table(y_back))

    planes = planes.reshape(n_px, CXP, n_pz, CYP, group).transpose(0, 2, 1, 3, 4)
    planes = planes.reshape(n_dev, CXP * CYP, group)
    turned = lax.all_to_all(planes, AXES, split_axis=0, concat_axis=0, tiled=True)
    spectrum = turned.reshape(n_px, n_pz, CXP * CYP, group).transpose(2, 1, 0, 3)
    spectrum = spectrum.reshape(CXP * CYP, 2 * NZP)
    phi = product("pk,zk->pz", spectrum, long) * (1.0 / (2 * NZP))
    back = pick("rb,bl->rl", placing, phi.reshape(pencil_blocks, 128)).reshape(n_dev, cap, 128)
    got = lax.all_to_all(back, AXES, split_axis=0, concat_axis=0, tiled=True)
    return pick("sr,rl->sl", packing, got.reshape(n_dev * cap, 128))


LANES = 128
GROUP = 64
KEPT = 8
HALF = 32
WIDE = 32
MESH = pl.DeviceIdType.MESH


def unit_rows(frequencies, is_sine, wide):
    period = 2 * wide
    angle = (frequencies[:, None] * np.arange(wide)[None, :] % period) * (2.0 * math.pi / period)
    weight = np.where((frequencies == 0) | (frequencies == wide), 1.0, 2.0) / period
    return np.where(is_sine[:, None], np.sin(angle), np.cos(angle)) * np.sqrt(weight)[:, None]


def folded_table():
    k = np.arange(2 * NZP)[None, :]
    frequency = np.minimum(k, 2 * NZP - k)
    odd = 2 * np.arange(NZP // 2)[:, None] - (NZP - 1)
    angle = (frequency * odd % (4 * NZP)) * (2.0 * math.pi / (4 * NZP))
    weight = np.where((frequency == 0) | (frequency == NZP), 1.0, 2.0) / (2 * NZP)
    return np.where(k < NZP, np.cos(angle), np.sin(angle)) * np.sqrt(weight)


def plane_tables(n_px, n_pz):
    y_tables = []
    for half in range(2):
        raw = half * WIDE + np.arange(HALF)
        folded = np.minimum(raw, 2 * WIDE - raw)
        lone = folded == folded[0]
        frequencies = np.concatenate((folded, np.where(lone, WIDE - folded[0], folded)))
        sine = np.concatenate((np.zeros(HALF, bool), ~lone))
        rows = unit_rows(frequencies, sine, WIDE).reshape(2 * n_px, KEPT, n_pz, CYP)
        table = np.einsum("gqjb,iI,aA->ijabgIqA", rows, np.eye(n_px), np.eye(4))
        y_tables.append(table.reshape(n_px * n_pz * 16, 2 * n_px * n_px * KEPT * 4))
    y_table = np.stack(y_tables)
    base = np.arange(HALF)
    frequencies = np.concatenate((base, np.where(base == 0, WIDE, base)))
    sine = np.concatenate((np.zeros(HALF, bool), base != 0))
    rows = unit_rows(frequencies, sine, WIDE).reshape(2 * HALF, n_px, 2, 4)
    x_table = np.einsum("uiha,qQ->hiqauQ", rows, np.eye(KEPT))
    x_table = x_table.reshape(2 * n_px * KEPT * 4, 2 * HALF * KEPT)
    return y_table, x_table


def halves(values):
    high = values.astype(jnp.bfloat16)
    return high, (values - high.astype(jnp.float32)).astype(jnp.bfloat16)


def mm(a, b, contract=((1,), (0,))):
    return lax.dot_general(a, b, (contract, ((), ())), preferred_element_type=jnp.float32)


def mm_left(values, high, low, contract=((1,), (0,))):
    v_high, v_low = halves(values)
    rows = values.shape[0]
    both = mm(jnp.concatenate((v_high, v_low), axis=0), high, contract)
    return both[:rows] + (both[rows:] + mm(v_high, low, contract))


def mm_pick(one_hot, values):
    high, low = halves(values)
    return mm(one_hot, high) + mm(one_hot, low)


def iota(shape, axis):
    return lax.broadcasted_iota(jnp.int32, shape, axis)


def as_row(column):
    return jnp.transpose(jnp.broadcast_to(column, (column.shape[0], LANES)))[0:1, :]


def as_column(row):
    return jnp.transpose(jnp.broadcast_to(row, (LANES, row.shape[1])))[:, 0:1]


def one(mask):
    return jnp.where(mask, 1.0, 0.0).astype(jnp.bfloat16)


def fused(
    n_px, n_pz, charge_ref, dest_ref, ids_ref, green_hbm, zh_hbm, zl_hbm, yh_hbm, yl_hbm, xh_hbm,
    xl_hbm, out_ref, green, zh, zl, yh, yl, xh, xl, ids_send, ids_recv, charge_send, charge_recv,
    green_send, green_recv, edge_recv, spec_send, spec_recv, back_send, back_recv, out_send, out_recv, scale, folded,
    load_sems, green_sems, send_sems, recv_sems
):
    n_dev = n_px * n_pz
    mi, mj = lax.axis_index("px"), lax.axis_index("pz")
    me = mi * n_pz + mj
    slots = charge_ref.shape[0]
    cap = charge_send.shape[1]
    rows = n_dev * cap
    side = n_dev // 2
    near = me // side
    far = 1 - near
    blocks = CXP * CYP * NZP // LANES

    barrier = pltpu.get_barrier_semaphore()

    def greet(step, carry):
        peer = lax.rem(me + step, n_dev)
        pl.semaphore_signal(
            barrier, inc=1, device_id=(peer // n_pz, lax.rem(peer, n_pz)), device_id_type=MESH
        )
        return carry

    lax.fori_loop(1, n_dev, greet, 0)

    loads = [
        pltpu.make_async_copy(source, target, load_sems.at[number])
        for number, (source, target) in enumerate((
            (green_hbm.at[pl.ds(0, 40)], green), (zh_hbm, zh), (zl_hbm, zl), (yh_hbm.at[near], yh),
            (yl_hbm.at[near], yl), (xh_hbm, xh), (xl_hbm, xl),
        ))
    ]
    for load in loads:
        load.start()

    def block_copy(send, recv, number, peer, part):
        return pltpu.make_async_remote_copy(
            src_ref=send.at[peer],
            dst_ref=recv.at[me],
            send_sem=send_sems.at[number],
            recv_sem=recv_sems.at[number, part],
            device_id=(peer // n_pz, lax.rem(peer, n_pz)),
            device_id_type=MESH,
        )

    def send_far(send, recv, number):
        def body(step, carry):
            block_copy(send, recv, number, far * side + lax.rem(me + step, side), 1).start()
            return carry

        lax.fori_loop(0, side, body, 0)

    def send_near(send, recv, number):
        def body(step, carry):
            block_copy(send, recv, number, near * side + lax.rem(me + step, side), 0).start()
            return carry

        lax.fori_loop(1, side, body, 0)
        recv[me] = send[me]

    def send_all(send, recv, number):
        send_far(send, recv, number)
        send_near(send, recv, number)

    def all_of(send, recv, number, count, part=0):
        return pltpu.make_async_remote_copy(
            src_ref=send.at[pl.ds(0, count)],
            dst_ref=recv.at[pl.ds(0, count)],
            send_sem=send_sems.at[number],
            recv_sem=recv_sems.at[number, part],
            device_id=(mi, mj),
            device_id_type=MESH,
        )

    def wait_near(send, recv, number):
        all_of(send, recv, number, side - 1, 0).wait_recv()

    def wait_far(send, recv, number):
        all_of(send, recv, number, side, 1).wait_recv()

    def wait_both(send, recv, number):
        wait_near(send, recv, number)
        wait_far(send, recv, number)

    dest_row = dest_ref[...].astype(jnp.float32)
    dest = as_column(dest_row)
    named = one(dest == iota((slots, LANES), 1).astype(jnp.float32))
    before = one(iota((slots, slots), 1) < iota((slots, slots), 0))
    rank = jnp.sum(mm(before, named) * named.astype(jnp.float32), axis=1, keepdims=True)
    place = dest * cap + rank
    ids = ids_ref[...].astype(jnp.float32) + 1.0
    owned = jnp.where(dest_row == iota((n_dev, slots), 0).astype(jnp.float32), ids, 0.0)
    ranked = one(rank == iota((slots, LANES), 1).astype(jnp.float32))
    ids_send[...] = mm(owned.astype(jnp.bfloat16), ranked).reshape(n_dev, 1, LANES)
    packing = one(as_row(place) == iota((rows, slots), 0).astype(jnp.float32))
    charge_send[...] = mm_pick(packing, charge_ref[...]).reshape(n_dev, cap, LANES)
    pl.semaphore_wait(barrier, n_dev - 1)
    send_all(ids_send, ids_recv, 0)
    send_all(charge_send, charge_recv, 1)

    loads[0].wait()
    wide = [jnp.transpose(green[0:HALF, t * KEPT : (t + 1) * KEPT, :].reshape(HALF * KEPT, 256)) for t in range(2)]
    edge = jnp.concatenate((green[HALF], green[0:40, 0, :], jnp.zeros((LANES - 56, 256), jnp.float32)), axis=0)
    green_send[...] = jnp.concatenate((*wide, jnp.transpose(edge)), axis=1).reshape(n_px, GROUP, 640)
    odd = lax.rem(mi, 2)
    partner = mi + 1 - 2 * odd
    green_copy = pltpu.make_async_remote_copy(
        src_ref=green_send.at[partner],
        dst_ref=green_recv.at[odd],
        send_sem=green_sems.at[0],
        recv_sem=green_sems.at[3],
        device_id=(partner, mj),
        device_id_type=MESH,
    )
    green_copy.start()

    def edge_copy(step):
        target = far * 2 + step
        return pltpu.make_async_remote_copy(
            src_ref=green_send.at[target, :, pl.ds(512, LANES)],
            dst_ref=edge_recv,
            send_sem=green_sems.at[1 + step],
            recv_sem=green_sems.at[4],
            device_id=(target, mj),
            device_id_type=MESH,
        )

    @pl.when(odd == 0)
    def _():
        for step in range(2):
            edge_copy(step).start()

    green_recv[odd] = green_send[mi]

    wait_both(ids_send, ids_recv, 0)
    line = iota((rows, n_dev), 0)
    spread = mm(one(line // cap == iota((rows, n_dev), 1)), ids_recv[...].reshape(n_dev, LANES).astype(jnp.bfloat16))
    own_lane = iota((rows, LANES), 1) == lax.rem(iota((rows, LANES), 0), cap)
    ids = jnp.sum(jnp.where(own_lane, spread, 0.0), axis=1, keepdims=True)
    lines = CXP * CYP

    def target_of(index):
        return (lax.rem(index, lines) * (NZP // LANES) + index // lines + 1).astype(jnp.float32)

    taking = one(ids == target_of(iota((rows, blocks), 1)))
    placing = one(as_row(ids) == target_of(iota((blocks, rows), 0)))
    wait_both(charge_send, charge_recv, 1)
    field = mm_pick(placing, charge_recv[...].reshape(rows, LANES))
    mirror = one(iota((LANES, LANES), 0) + iota((LANES, LANES), 1) == LANES - 1)
    pieces_z = NZP // LANES
    middle = lines * pieces_z // 2
    front = field[:middle]
    m_high, m_low = halves(field[middle:])
    rear = mm(m_high, mirror) + mm(m_low, mirror)
    front = jnp.concatenate([front[lines * c : lines * (c + 1)] for c in range(pieces_z // 2)], axis=1)
    rear = jnp.concatenate(
        [rear[lines * c : lines * (c + 1)] for c in range(pieces_z // 2 - 1, -1, -1)], axis=1
    )

    for odd_part, part in enumerate((front + rear, front - rear)):
        folded[odd_part] = jnp.concatenate(halves(part), axis=0)
    loads[1].wait()
    loads[2].wait()
    first = iota((lines // 2, LANES), 1) < GROUP

    def forward(half, part):
        def body(step, carry):
            two = lax.rem(mj // 2 + step, n_pz // 2)
            columns = pl.ds(pl.multiple_of(half * NZP + two * 256, 256), 256)
            part_of = folded[two // (n_pz // 4)]
            both = mm(part_of, zh[:, columns])
            total = both[:lines] + (both[lines:] + mm(part_of[:lines], zl[:, columns]))
            for t in range(2):
                j = two * 2 + t
                tile = total[:, t * LANES : (t + 1) * LANES]
                low, high = tile[: lines // 2], tile[lines // 2 :]
                low_turned, high_turned = pltpu.roll(low, GROUP, 1), pltpu.roll(high, GROUP, 1)
                at = half * side + j
                spec_send[at] = jnp.where(first, low, high_turned)
                spec_send[at + n_pz] = jnp.where(first, low_turned, high)
                for peer in (at, at + n_pz):
                    if part == 1:
                        block_copy(spec_send, spec_recv, 3, peer, 1).start()
                    else:

                        @pl.when(peer != me)
                        def _():
                            block_copy(spec_send, spec_recv, 3, peer, 0).start()

            return carry

        lax.fori_loop(0, n_pz // 2, body, 0)

    forward(far, 1)
    forward(near, 0)
    spec_recv[me] = spec_send[me]

    green_copy.wait_recv()
    edge_copy(0).wait_recv()
    source, target = iota((LANES, 512), 0), iota((LANES, 512), 1)
    wanted = jnp.where(target == 256, HALF, lax.rem(target, 256) // KEPT) + 2 * KEPT
    picking = one((source == wanted) & (lax.rem(target, KEPT) == 0))
    e_high, e_low = halves(edge_recv[...])
    lone = mm(e_high, picking) + mm(e_low, picking)
    lane = iota((GROUP, LANES), 1)
    for parity in range(2):
        edge = green_recv[parity, :, 512:640]
        for t in range(2):
            wide = green_recv[parity, :, t * 256 : (t + 1) * 256]
            turned = edge if t == 0 else pltpu.roll(edge, LANES - KEPT, 1)
            start = jnp.where(lane < KEPT, turned, wide[:, :LANES])
            full = jnp.concatenate((wide, start, wide[:, LANES:]), axis=1)
            at = (2 * parity + t) * GROUP
            scale[at : at + GROUP, :] = full
            if parity == 0 and t == 0:
                full = jnp.where(lax.rem(iota((GROUP, 512), 1), KEPT) == 0, lone, full)
            at = at + n_px * GROUP
            scale[at : at + GROUP, :] = full

    for load in loads[3:]:
        load.wait()

    def side_planes(half):
        taken = spec_recv[pl.ds(half * side, side)].reshape(side * 16, LANES)
        table_rows = pl.ds(pl.multiple_of(half * (side * 16), side * 16), side * 16)
        return mm_left(jnp.transpose(taken), yh[table_rows, :], yl[table_rows, :])

    wait_near(spec_send, spec_recv, 3)
    planes = side_planes(near)
    wait_far(spec_send, spec_recv, 3)
    planes = planes + side_planes(far)
    groups = 2 * n_px
    planes = jnp.concatenate(
        [
            jnp.concatenate(
                [planes[h * GROUP : (h + 1) * GROUP, g * LANES : (g + 1) * LANES] for h in range(2)], axis=1
            )
            for g in range(groups)
        ],
        axis=0,
    )
    planes = mm_left(planes, xh[...], xl[...]) * scale[...]
    planes = mm_left(planes, xh[...], xl[...], ((1,), (1,)))
    planes = jnp.concatenate(
        [
            jnp.concatenate(
                [planes[g * GROUP : (g + 1) * GROUP, h * LANES : (h + 1) * LANES] for g in range(groups)], axis=1
            )
            for h in range(2)
        ],
        axis=0,
    )
    p_high, p_low = halves(planes)
    right = ((1,), (1,))

    def side_back(half):
        table_rows = pl.ds(pl.multiple_of(half * (side * 16), side * 16), side * 16)
        high, low = yh[table_rows, :], yl[table_rows, :]
        given = mm(high, p_high, right) + (mm(high, p_low, right) + mm(low, p_high, right))
        back_send[pl.ds(half * side, side)] = given.reshape(side, 16, LANES)

    side_back(far)
    send_far(back_send, back_recv, 4)
    side_back(near)
    send_near(back_send, back_recv, 4)

    def side_phi(half):
        pieces = []
        for j in range(n_pz):
            left, other = back_recv[half * side + j], back_recv[half * side + n_pz + j]
            low = jnp.where(first, left, pltpu.roll(other, GROUP, 1))
            high = jnp.where(first, pltpu.roll(left, GROUP, 1), other)
            pieces.append(jnp.concatenate((low, high), axis=0))
        given = []
        for odd_part in range(2):
            columns = pl.ds(pl.multiple_of(half * NZP + odd_part * (NZP // 2), NZP // 2), NZP // 2)
            group = pieces[odd_part * n_pz // 2 : (odd_part + 1) * n_pz // 2]
            given.append(mm_left(jnp.concatenate(group, axis=1), zh[:, columns], zl[:, columns], right))
        return given

    wait_near(back_send, back_recv, 4)
    near_phi = side_phi(near)
    wait_far(back_send, back_recv, 4)
    even, odd_sum = [one_side + other for one_side, other in zip(near_phi, side_phi(far))]
    front, rear = even + odd_sum, even - odd_sum
    front = [front[:, c * LANES : (c + 1) * LANES] for c in range(pieces_z // 2)]
    rear = [rear[:, c * LANES : (c + 1) * LANES] for c in range(pieces_z // 2 - 1, -1, -1)]
    m_high, m_low = halves(jnp.concatenate(rear, axis=0))
    phi = jnp.concatenate((*front, mm(m_high, mirror) + mm(m_low, mirror)), axis=0)
    out_send[...] = mm_pick(taking, phi).reshape(n_dev, cap, LANES)
    send_all(out_send, out_recv, 5)
    unpacking = one(place == iota((slots, rows), 1).astype(jnp.float32))
    wait_both(out_send, out_recv, 5)
    out_ref[...] = mm_pick(unpacking, out_recv[...].reshape(rows, LANES))

    all_of(ids_send, ids_recv, 0, n_dev - 1).wait_send()
    all_of(charge_send, charge_recv, 1, n_dev - 1).wait_send()
    green_copy.wait_send()

    @pl.when(odd == 0)
    def _():
        for step in range(2):
            edge_copy(step).wait_send()

    all_of(spec_send, spec_recv, 3, n_dev - 1).wait_send()
    all_of(back_send, back_recv, 4, n_dev - 1).wait_send()
    all_of(out_send, out_recv, 5, n_dev - 1).wait_send()


def local_fused(charge, dest, local_ids, green_hat):
    n_px, n_pz = lax.axis_size("px"), lax.axis_size("pz")
    n_dev = n_px * n_pz
    slots = charge.shape[0]
    cap = 2 * slots // n_dev
    y_table, x_table = plane_tables(n_px, n_pz)
    z_table = folded_table().reshape(NZP // 2, n_pz, 2, 2 * GROUP).transpose(0, 2, 1, 3)
    z_table = z_table.reshape(NZP // 2, 2 * NZP)
    tables = [
        piece
        for table in (z_table, y_table, x_table)
        for piece in split_table(table)
    ]
    exchange = lambda lead, rows: [pltpu.VMEM((lead, rows, LANES), jnp.float32)] * 2
    vmem, anywhere = pl.BlockSpec(memory_space=pltpu.VMEM), pl.BlockSpec(memory_space=pltpu.HBM)
    return pl.pallas_call(
        functools.partial(fused, n_px, n_pz),
        out_shape=jax.ShapeDtypeStruct(charge.shape, jnp.float32),
        in_specs=[vmem] * 3 + [anywhere] * 7,
        out_specs=vmem,
        scratch_shapes=[
            pltpu.VMEM((40,) + green_hat.shape[1:], jnp.float32),
            *[pltpu.VMEM(table.shape[-2:], jnp.bfloat16) for table in tables],
            *exchange(n_dev, 1),
            *exchange(n_dev, cap),
            pltpu.VMEM((n_px, GROUP, 640), jnp.float32),
            pltpu.VMEM((2, GROUP, 640), jnp.float32),
            pltpu.VMEM((GROUP, LANES), jnp.float32),
            *exchange(n_dev, 16),
            *exchange(n_dev, 16),
            *exchange(n_dev, cap),
            pltpu.VMEM((2 * n_px * GROUP, 2 * HALF * KEPT), jnp.float32),
            pltpu.VMEM((2, 2 * CXP * CYP, NZP // 2), jnp.bfloat16),
            pltpu.SemaphoreType.DMA((7,)),
            pltpu.SemaphoreType.DMA((5,)),
            pltpu.SemaphoreType.DMA((6,)),
            pltpu.SemaphoreType.DMA((6, 2)),
        ],
        compiler_params=pltpu.CompilerParams(
            collective_id=0, has_side_effects=True, vmem_limit_bytes=64 * 1024 * 1024
        ),
    )(charge, dest.reshape(1, slots), local_ids.reshape(1, slots), green_hat, *tables)


def solution(mesh):
    planes = mesh.shape["px"] == 4 and mesh.shape["pz"] == 8
    return jax.shard_map(
        local_fused if planes else local,
        mesh=mesh,
        in_specs=(
            P(AXES, None),
            P(AXES, None),
            P(AXES),
            P(None, "px", "pz"),
        ),
        out_specs=P(AXES, None),
        check_vma=False,
    )
```

```python
import functools
import math

import jax
import jax.numpy as jnp
import numpy as np
from jax import lax
from jax.experimental import pallas as pl
from jax.experimental.pallas import tpu as pltpu
from jax.sharding import PartitionSpec as P

CXP = 8
CYP = 4
NZP = 1024
AXES = ("px", "pz")


def split_table(table):
    high = table.astype(np.float32).astype(jnp.bfloat16)
    low = (table - high.astype(np.float64)).astype(np.float32).astype(jnp.bfloat16)
    return np.asarray(high), np.asarray(low)


def long_table():
    n = np.arange(NZP)[:, None]
    k = np.arange(2 * NZP)[None, :]
    angle = (n * k % (2 * NZP)) * (2.0 * math.pi / (2 * NZP))
    return np.cos(angle) + np.sin(angle)


def short_tables(wide, frequencies):
    period = 2 * wide
    folded = np.minimum(frequencies, period - frequencies)
    angle = (frequencies[:, None] * np.arange(wide)[None, :] % period) * (2.0 * math.pi / period)
    table = np.concatenate((np.cos(angle), np.sin(angle)), axis=0)
    weight = np.where((folded == 0) | (folded == wide), 1.0, 2.0) / period
    count = np.array([(folded == f).sum() for f in folded])
    weight = np.tile(weight / count, 2)
    return table, table * weight[:, None]


def split(values):
    high = lax.reduce_precision(values, 8, 7)
    return high.astype(jnp.bfloat16), (values - high).astype(jnp.bfloat16)


def product(form, values, table):
    high, low = split(values)
    t_high, t_low = table
    dot = lambda a, b: jnp.einsum(form, a, b, preferred_element_type=jnp.float32)
    return dot(high, t_high) + (dot(low, t_high) + dot(high, t_low))


def pick(form, one_hot, values):
    high, low = split(values)
    dot = lambda b: jnp.einsum(form, one_hot, b, preferred_element_type=jnp.float32)
    return dot(high) + dot(low)


def kept_frequencies(wide_y, n_px):
    own = 2 * wide_y // n_px
    return (np.arange(n_px)[:, None] * own + np.arange(own // 2 + 1)[None, :]).reshape(-1)


def local(charge, dest, local_ids, green_hat):
    n_px = lax.axis_size("px")
    n_pz = lax.axis_size("pz")
    n_dev = n_px * n_pz
    wide_x, wide_y = CXP * n_px, CYP * n_pz
    slots = charge.shape[0]
    cap = 2 * slots // n_dev
    pencil_blocks = CXP * CYP * NZP // 128
    own = 2 * wide_y // n_px
    group = 2 * NZP // n_dev

    green = lax.all_to_all(
        green_hat[: wide_x + 1, : own // 2 + 1], "px", split_axis=2, concat_axis=1, tiled=True
    )

    route = dest[:, 0]
    named = (route[:, None] == jnp.arange(n_dev)[None, :]).astype(jnp.bfloat16)
    before = jnp.asarray(np.tril(np.ones((slots, slots)), -1), jnp.bfloat16)
    rank = jnp.sum(
        jnp.einsum("st,td->sd", before, named, preferred_element_type=jnp.float32) * named, axis=1
    ).astype(jnp.int32)
    place = route * cap + rank
    packing = (place[:, None] == jnp.arange(n_dev * cap)[None, :]).astype(jnp.bfloat16)
    sent = pick("sr,sl->rl", packing, charge).reshape(n_dev, cap, 128)
    ids = jnp.einsum(
        "sr,s->r", packing, (local_ids + 1).astype(jnp.bfloat16), preferred_element_type=jnp.float32
    ).reshape(n_dev, 1, cap)
    sent = jnp.concatenate((sent, jnp.pad(ids, ((0, 0), (0, 0), (0, 128 - cap)))), axis=1)
    got = lax.all_to_all(sent, AXES, split_axis=0, concat_axis=0, tiled=True)
    ids = got[:, cap, :cap].reshape(n_dev * cap).astype(jnp.int32) - 1
    placing = (ids[:, None] == jnp.arange(pencil_blocks)[None, :]).astype(jnp.bfloat16)
    field = pick("rb,rl->bl", placing, got[:, :cap].reshape(n_dev * cap, 128))
    field = field.reshape(CXP * CYP, NZP)

    long = split_table(long_table())
    spectrum = product("pz,zk->pk", field, long)
    spectrum = spectrum.reshape(CXP * CYP, n_pz, n_px, group).transpose(2, 1, 0, 3)
    spectrum = spectrum.reshape(n_dev, CXP * CYP, group)
    turned = lax.all_to_all(spectrum, AXES, split_axis=0, concat_axis=0, tiled=True)
    planes = turned.reshape(n_px, n_pz, CXP, CYP, group).transpose(0, 2, 1, 3, 4)
    planes = planes.reshape(wide_x, wide_y, group)

    kept_y = kept_frequencies(wide_y, n_px)
    y_table, y_back = short_tables(wide_y, kept_y)
    x_table, x_back = short_tables(wide_x, np.arange(wide_x + 1))
    planes = product("xyk,qy->xqk", planes, split_table(y_table))
    planes = product("xqk,ux->uqk", planes, split_table(x_table))
    count_x, count_y = wide_x + 1, len(kept_y)
    planes = planes.reshape(2, count_x, 2, count_y, group) * green[None, :, None]
    planes = planes.reshape(2 * count_x, 2 * count_y, group)
    planes = product("uqk,ux->xqk", planes, split_table(x_back))
    planes = product("xqk,qy->xyk", planes, split_table(y_back))

    planes = planes.reshape(n_px, CXP, n_pz, CYP, group).transpose(0, 2, 1, 3, 4)
    planes = planes.reshape(n_dev, CXP * CYP, group)
    turned = lax.all_to_all(planes, AXES, split_axis=0, concat_axis=0, tiled=True)
    spectrum = turned.reshape(n_px, n_pz, CXP * CYP, group).transpose(2, 1, 0, 3)
    spectrum = spectrum.reshape(CXP * CYP, 2 * NZP)
    phi = product("pk,zk->pz", spectrum, long) * (1.0 / (2 * NZP))
    back = pick("rb,bl->rl", placing, phi.reshape(pencil_blocks, 128)).reshape(n_dev, cap, 128)
    got = lax.all_to_all(back, AXES, split_axis=0, concat_axis=0, tiled=True)
    return pick("sr,rl->sl", packing, got.reshape(n_dev * cap, 128))


LANES = 128
GROUP = 64
KEPT = 8
HALF = 32
WIDE = 32
MESH = pl.DeviceIdType.MESH


def unit_rows(frequencies, is_sine, wide):
    period = 2 * wide
    angle = (frequencies[:, None] * np.arange(wide)[None, :] % period) * (2.0 * math.pi / period)
    weight = np.where((frequencies == 0) | (frequencies == wide), 1.0, 2.0) / period
    return np.where(is_sine[:, None], np.sin(angle), np.cos(angle)) * np.sqrt(weight)[:, None]


def folded_table():
    k = np.arange(2 * NZP)[None, :]
    frequency = np.minimum(k, 2 * NZP - k)
    odd = 2 * np.arange(NZP // 2)[:, None] - (NZP - 1)
    angle = (frequency * odd % (4 * NZP)) * (2.0 * math.pi / (4 * NZP))
    weight = np.where((frequency == 0) | (frequency == NZP), 1.0, 2.0) / (2 * NZP)
    return np.where(k < NZP, np.cos(angle), np.sin(angle)) * np.sqrt(weight)


def plane_tables(n_px, n_pz):
    y_tables = []
    for half in range(2):
        raw = half * WIDE + np.arange(HALF)
        folded = np.minimum(raw, 2 * WIDE - raw)
        lone = folded == folded[0]
        frequencies = np.concatenate((folded, np.where(lone, WIDE - folded[0], folded)))
        sine = np.concatenate((np.zeros(HALF, bool), ~lone))
        rows = unit_rows(frequencies, sine, WIDE).reshape(2 * n_px, KEPT, n_pz, CYP)
        table = np.einsum("gqjb,iI,aA->ijabgIqA", rows, np.eye(n_px), np.eye(4))
        y_tables.append(table.reshape(n_px * n_pz * 16, 2 * n_px * n_px * KEPT * 4))
    y_table = np.stack(y_tables)
    base = np.arange(HALF)
    frequencies = np.concatenate((base, np.where(base == 0, WIDE, base)))
    sine = np.concatenate((np.zeros(HALF, bool), base != 0))
    rows = unit_rows(frequencies, sine, WIDE).reshape(2 * HALF, n_px, 2, 4)
    x_table = np.einsum("uiha,qQ->hiqauQ", rows, np.eye(KEPT))
    x_table = x_table.reshape(2 * n_px * KEPT * 4, 2 * HALF * KEPT)
    return y_table, x_table


def halves(values):
    high = values.astype(jnp.bfloat16)
    return high, (values - high.astype(jnp.float32)).astype(jnp.bfloat16)


def mm(a, b, contract=((1,), (0,))):
    return lax.dot_general(a, b, (contract, ((), ())), preferred_element_type=jnp.float32)


def mm_left(values, high, low, contract=((1,), (0,))):
    v_high, v_low = halves(values)
    rows = values.shape[0]
    both = mm(jnp.concatenate((v_high, v_low), axis=0), high, contract)
    return both[:rows] + (both[rows:] + mm(v_high, low, contract))


def mm_pick(one_hot, values):
    high, low = halves(values)
    return mm(one_hot, high) + mm(one_hot, low)


def iota(shape, axis):
    return lax.broadcasted_iota(jnp.int32, shape, axis)


def as_row(column):
    return jnp.transpose(jnp.broadcast_to(column, (column.shape[0], LANES)))[0:1, :]


def as_column(row):
    return jnp.transpose(jnp.broadcast_to(row, (LANES, row.shape[1])))[:, 0:1]


def one(mask):
    return jnp.where(mask, 1.0, 0.0).astype(jnp.bfloat16)


def fused(
    n_px, n_pz, charge_ref, dest_ref, ids_ref, green_hbm, zh_hbm, zl_hbm, yh_hbm, yl_hbm, xh_hbm,
    xl_hbm, out_ref, green, zh, zl, yh, yl, xh, xl, ids_send, ids_recv, charge_send, charge_recv,
    green_send, green_recv, edge_recv, spec_send, spec_recv, back_send, back_recv, out_send, out_recv, scale, folded,
    load_sems, green_sems, send_sems, recv_sems
):
    n_dev = n_px * n_pz
    mi, mj = lax.axis_index("px"), lax.axis_index("pz")
    me = mi * n_pz + mj
    slots = charge_ref.shape[0]
    cap = charge_send.shape[1]
    rows = n_dev * cap
    side = n_dev // 2
    near = me // side
    far = 1 - near
    blocks = CXP * CYP * NZP // LANES

    barrier = pltpu.get_barrier_semaphore()

    def greet(step, carry):
        peer = lax.rem(me + step, n_dev)
        pl.semaphore_signal(
            barrier, inc=1, device_id=(peer // n_pz, lax.rem(peer, n_pz)), device_id_type=MESH
        )
        return carry

    lax.fori_loop(1, n_dev, greet, 0)

    loads = [
        pltpu.make_async_copy(source, target, load_sems.at[number])
        for number, (source, target) in enumerate((
            (green_hbm.at[pl.ds(0, 40)], green), (zh_hbm, zh), (zl_hbm, zl), (yh_hbm.at[near], yh),
            (yl_hbm.at[near], yl), (xh_hbm, xh), (xl_hbm, xl),
        ))
    ]
    for load in loads:
        load.start()

    def block_copy(send, recv, number, peer, part):
        return pltpu.make_async_remote_copy(
            src_ref=send.at[peer],
            dst_ref=recv.at[me],
            send_sem=send_sems.at[number],
            recv_sem=recv_sems.at[number, part],
            device_id=(peer // n_pz, lax.rem(peer, n_pz)),
            device_id_type=MESH,
        )

    def send_far(send, recv, number):
        def body(step, carry):
            block_copy(send, recv, number, far * side + lax.rem(me + step, side), 1).start()
            return carry

        lax.fori_loop(0, side, body, 0)

    def send_near(send, recv, number):
        def body(step, carry):
            block_copy(send, recv, number, near * side + lax.rem(me + step, side), 0).start()
            return carry

        lax.fori_loop(1, side, body, 0)
        recv[me] = send[me]

    def send_all(send, recv, number):
        def body(step, carry):
            block_copy(send, recv, number, far * side + lax.rem(me + step, side), 1).start()
            block_copy(send, recv, number, near * side + lax.rem(me + step, side), 0).start()
            return carry

        block_copy(send, recv, number, far * side + lax.rem(me, side), 1).start()
        lax.fori_loop(1, side, body, 0)
        recv[me] = send[me]

    def all_of(send, recv, number, count, part=0):
        return pltpu.make_async_remote_copy(
            src_ref=send.at[pl.ds(0, count)],
            dst_ref=recv.at[pl.ds(0, count)],
            send_sem=send_sems.at[number],
            recv_sem=recv_sems.at[number, part],
            device_id=(mi, mj),
            device_id_type=MESH,
        )

    def wait_near(send, recv, number):
        all_of(send, recv, number, side - 1, 0).wait_recv()

    def wait_far(send, recv, number):
        all_of(send, recv, number, side, 1).wait_recv()

    def wait_both(send, recv, number):
        wait_near(send, recv, number)
        wait_far(send, recv, number)

    dest_row = dest_ref[...].astype(jnp.float32)
    dest = as_column(dest_row)
    named = one(dest == iota((slots, LANES), 1).astype(jnp.float32))
    before = one(iota((slots, slots), 1) < iota((slots, slots), 0))
    rank = jnp.sum(mm(before, named) * named.astype(jnp.float32), axis=1, keepdims=True)
    place = dest * cap + rank
    ids = ids_ref[...].astype(jnp.float32) + 1.0
    owned = jnp.where(dest_row == iota((n_dev, slots), 0).astype(jnp.float32), ids, 0.0)
    ranked = one(rank == iota((slots, LANES), 1).astype(jnp.float32))
    ids_send[...] = mm(owned.astype(jnp.bfloat16), ranked).reshape(n_dev, 1, LANES)
    packing = one(as_row(place) == iota((rows, slots), 0).astype(jnp.float32))
    charge_send[...] = mm_pick(packing, charge_ref[...]).reshape(n_dev, cap, LANES)
    pl.semaphore_wait(barrier, n_dev - 1)
    send_all(ids_send, ids_recv, 0)
    send_all(charge_send, charge_recv, 1)

    loads[0].wait()
    wide = [jnp.transpose(green[0:HALF, t * KEPT : (t + 1) * KEPT, :].reshape(HALF * KEPT, 256)) for t in range(2)]
    edge = jnp.concatenate((green[HALF], green[0:40, 0, :], jnp.zeros((LANES - 56, 256), jnp.float32)), axis=0)
    green_send[...] = jnp.concatenate((*wide, jnp.transpose(edge)), axis=1).reshape(n_px, GROUP, 640)
    odd = lax.rem(mi, 2)
    partner = mi + 1 - 2 * odd
    green_copy = pltpu.make_async_remote_copy(
        src_ref=green_send.at[partner],
        dst_ref=green_recv.at[odd],
        send_sem=green_sems.at[0],
        recv_sem=green_sems.at[3],
        device_id=(partner, mj),
        device_id_type=MESH,
    )
    green_copy.start()

    def edge_copy(step):
        target = far * 2 + step
        return pltpu.make_async_remote_copy(
            src_ref=green_send.at[target, :, pl.ds(512, LANES)],
            dst_ref=edge_recv,
            send_sem=green_sems.at[1 + step],
            recv_sem=green_sems.at[4],
            device_id=(target, mj),
            device_id_type=MESH,
        )

    @pl.when(odd == 0)
    def _():
        for step in range(2):
            edge_copy(step).start()

    green_recv[odd] = green_send[mi]

    wait_both(ids_send, ids_recv, 0)
    line = iota((rows, 1), 0)
    cap_bits, line_bits = cap.bit_length() - 1, (CXP * CYP).bit_length() - 1
    from_box = one((line >> cap_bits) == iota((1, n_dev), 1))
    spread = mm(from_box, ids_recv[...].reshape(n_dev, LANES).astype(jnp.bfloat16))
    own_lane = (line & (cap - 1)) == iota((1, LANES), 1)
    ids = jnp.sum(jnp.where(own_lane, spread, 0.0), axis=1, keepdims=True)
    lines = CXP * CYP

    def target_of(index):
        return ((index & (lines - 1)) * (NZP // LANES) + (index >> line_bits) + 1).astype(jnp.float32)

    taking = one(ids == target_of(iota((1, blocks), 1)))
    placing = one(as_row(ids) == target_of(iota((blocks, 1), 0)))
    wait_both(charge_send, charge_recv, 1)
    field = mm_pick(placing, charge_recv[...].reshape(rows, LANES))
    mirror = one(iota((LANES, LANES), 0) + iota((LANES, LANES), 1) == LANES - 1)
    pieces_z = NZP // LANES
    middle = lines * pieces_z // 2
    front = field[:middle]
    m_high, m_low = halves(field[middle:])
    rear = mm(m_high, mirror) + mm(m_low, mirror)
    front = jnp.concatenate([front[lines * c : lines * (c + 1)] for c in range(pieces_z // 2)], axis=1)
    rear = jnp.concatenate(
        [rear[lines * c : lines * (c + 1)] for c in range(pieces_z // 2 - 1, -1, -1)], axis=1
    )

    for odd_part, part in enumerate((front + rear, front - rear)):
        folded[odd_part] = jnp.concatenate(halves(part), axis=0)
    loads[1].wait()
    loads[2].wait()
    first = iota((lines // 2, LANES), 1) < GROUP

    def forward(half, part):
        def body(step, carry):
            two = lax.rem(mj // 2 + step, n_pz // 2)
            columns = pl.ds(pl.multiple_of(half * NZP + two * 256, 256), 256)
            part_of = folded[two // (n_pz // 4)]
            both = mm(part_of, zh[:, columns])
            total = both[:lines] + (both[lines:] + mm(part_of[:lines], zl[:, columns]))
            for t in range(2):
                j = two * 2 + t
                tile = total[:, t * LANES : (t + 1) * LANES]
                low, high = tile[: lines // 2], tile[lines // 2 :]
                low_turned, high_turned = pltpu.roll(low, GROUP, 1), pltpu.roll(high, GROUP, 1)
                at = half * side + j
                spec_send[at] = jnp.where(first, low, high_turned)
                spec_send[at + n_pz] = jnp.where(first, low_turned, high)
                for peer in (at, at + n_pz):
                    if part == 1:
                        block_copy(spec_send, spec_recv, 3, peer, 1).start()
                    else:

                        @pl.when(peer != me)
                        def _():
                            block_copy(spec_send, spec_recv, 3, peer, 0).start()

            return carry

        lax.fori_loop(0, n_pz // 2, body, 0)

    forward(near, 0)
    forward(far, 1)
    spec_recv[me] = spec_send[me]

    green_copy.wait_recv()
    edge_copy(0).wait_recv()
    target = iota((1, 512), 1)
    wanted = jnp.where(target == 256, HALF, (target & 255) >> 3) + 2 * KEPT
    wanted = jnp.where((target & (KEPT - 1)) == 0, wanted, -1)
    picking = one(iota((LANES, 1), 0) == wanted)
    e_high, e_low = halves(edge_recv[...])
    lone = mm(e_high, picking) + mm(e_low, picking)
    lane = iota((GROUP, LANES), 1)
    for parity in range(2):
        edge = green_recv[parity, :, 512:640]
        for t in range(2):
            wide = green_recv[parity, :, t * 256 : (t + 1) * 256]
            turned = edge if t == 0 else pltpu.roll(edge, LANES - KEPT, 1)
            start = jnp.where(lane < KEPT, turned, wide[:, :LANES])
            full = jnp.concatenate((wide, start, wide[:, LANES:]), axis=1)
            at = (2 * parity + t) * GROUP
            scale[at : at + GROUP, :] = full
            if parity == 0 and t == 0:
                full = jnp.where((target & (KEPT - 1)) == 0, lone, full)
            at = at + n_px * GROUP
            scale[at : at + GROUP, :] = full

    for load in loads[3:]:
        load.wait()

    def side_planes(half):
        taken = spec_recv[pl.ds(half * side, side)].reshape(side * 16, LANES)
        table_rows = pl.ds(pl.multiple_of(half * (side * 16), side * 16), side * 16)
        return mm_left(jnp.transpose(taken), yh[table_rows, :], yl[table_rows, :])

    wait_near(spec_send, spec_recv, 3)
    planes = side_planes(near)
    wait_far(spec_send, spec_recv, 3)
    planes = planes + side_planes(far)
    groups = 2 * n_px
    planes = jnp.concatenate(
        [
            jnp.concatenate(
                [planes[h * GROUP : (h + 1) * GROUP, g * LANES : (g + 1) * LANES] for h in range(2)], axis=1
            )
            for g in range(groups)
        ],
        axis=0,
    )
    planes = mm_left(planes, xh[...], xl[...]) * scale[...]
    planes = mm_left(planes, xh[...], xl[...], ((1,), (1,)))
    planes = jnp.concatenate(
        [
            jnp.concatenate(
                [planes[g * GROUP : (g + 1) * GROUP, h * LANES : (h + 1) * LANES] for g in range(groups)], axis=1
            )
            for h in range(2)
        ],
        axis=0,
    )
    p_high, p_low = halves(planes)
    right = ((1,), (1,))

    def side_back(half):
        table_rows = pl.ds(pl.multiple_of(half * (side * 16), side * 16), side * 16)
        high, low = yh[table_rows, :], yl[table_rows, :]
        given = mm(high, p_high, right) + (mm(high, p_low, right) + mm(low, p_high, right))
        back_send[pl.ds(half * side, side)] = given.reshape(side, 16, LANES)

    side_back(near)
    send_near(back_send, back_recv, 4)
    side_back(far)
    send_far(back_send, back_recv, 4)

    def side_phi(half):
        pieces = []
        for j in range(n_pz):
            left, other = back_recv[half * side + j], back_recv[half * side + n_pz + j]
            low = jnp.where(first, left, pltpu.roll(other, GROUP, 1))
            high = jnp.where(first, pltpu.roll(left, GROUP, 1), other)
            pieces.append(jnp.concatenate((low, high), axis=0))
        given = []
        for odd_part in range(2):
            columns = pl.ds(pl.multiple_of(half * NZP + odd_part * (NZP // 2), NZP // 2), NZP // 2)
            group = pieces[odd_part * n_pz // 2 : (odd_part + 1) * n_pz // 2]
            given.append(mm_left(jnp.concatenate(group, axis=1), zh[:, columns], zl[:, columns], right))
        return given

    wait_near(back_send, back_recv, 4)
    near_phi = side_phi(near)
    wait_far(back_send, back_recv, 4)
    even, odd_sum = [one_side + other for one_side, other in zip(near_phi, side_phi(far))]
    front, rear = even + odd_sum, even - odd_sum
    front = [front[:, c * LANES : (c + 1) * LANES] for c in range(pieces_z // 2)]
    rear = [rear[:, c * LANES : (c + 1) * LANES] for c in range(pieces_z // 2 - 1, -1, -1)]
    m_high, m_low = halves(jnp.concatenate(rear, axis=0))
    phi = jnp.concatenate((*front, mm(m_high, mirror) + mm(m_low, mirror)), axis=0)
    out_send[...] = mm_pick(taking, phi).reshape(n_dev, cap, LANES)
    send_all(out_send, out_recv, 5)
    unpacking = one(place == iota((slots, rows), 1).astype(jnp.float32))
    wait_both(out_send, out_recv, 5)
    out_ref[...] = mm_pick(unpacking, out_recv[...].reshape(rows, LANES))

    all_of(ids_send, ids_recv, 0, n_dev - 1).wait_send()
    all_of(charge_send, charge_recv, 1, n_dev - 1).wait_send()
    green_copy.wait_send()

    @pl.when(odd == 0)
    def _():
        for step in range(2):
            edge_copy(step).wait_send()

    all_of(spec_send, spec_recv, 3, n_dev - 1).wait_send()
    all_of(back_send, back_recv, 4, n_dev - 1).wait_send()
    all_of(out_send, out_recv, 5, n_dev - 1).wait_send()


def local_fused(charge, dest, local_ids, green_hat):
    n_px, n_pz = lax.axis_size("px"), lax.axis_size("pz")
    n_dev = n_px * n_pz
    slots = charge.shape[0]
    cap = 2 * slots // n_dev
    y_table, x_table = plane_tables(n_px, n_pz)
    z_table = folded_table().reshape(NZP // 2, n_pz, 2, 2 * GROUP).transpose(0, 2, 1, 3)
    z_table = z_table.reshape(NZP // 2, 2 * NZP)
    tables = [
        piece
        for table in (z_table, y_table, x_table)
        for piece in split_table(table)
    ]
    exchange = lambda lead, rows: [pltpu.VMEM((lead, rows, LANES), jnp.float32)] * 2
    vmem, anywhere = pl.BlockSpec(memory_space=pltpu.VMEM), pl.BlockSpec(memory_space=pltpu.HBM)
    return pl.pallas_call(
        functools.partial(fused, n_px, n_pz),
        out_shape=jax.ShapeDtypeStruct(charge.shape, jnp.float32),
        in_specs=[vmem] * 3 + [anywhere] * 7,
        out_specs=vmem,
        scratch_shapes=[
            pltpu.VMEM((40,) + green_hat.shape[1:], jnp.float32),
            *[pltpu.VMEM(table.shape[-2:], jnp.bfloat16) for table in tables],
            *exchange(n_dev, 1),
            *exchange(n_dev, cap),
            pltpu.VMEM((n_px, GROUP, 640), jnp.float32),
            pltpu.VMEM((2, GROUP, 640), jnp.float32),
            pltpu.VMEM((GROUP, LANES), jnp.float32),
            *exchange(n_dev, 16),
            *exchange(n_dev, 16),
            *exchange(n_dev, cap),
            pltpu.VMEM((2 * n_px * GROUP, 2 * HALF * KEPT), jnp.float32),
            pltpu.VMEM((2, 2 * CXP * CYP, NZP // 2), jnp.bfloat16),
            pltpu.SemaphoreType.DMA((7,)),
            pltpu.SemaphoreType.DMA((5,)),
            pltpu.SemaphoreType.DMA((6,)),
            pltpu.SemaphoreType.DMA((6, 2)),
        ],
        compiler_params=pltpu.CompilerParams(
            collective_id=0, has_side_effects=True, vmem_limit_bytes=64 * 1024 * 1024
        ),
    )(charge, dest.reshape(1, slots), local_ids.reshape(1, slots), green_hat, *tables)


def solution(mesh):
    planes = mesh.shape["px"] == 4 and mesh.shape["pz"] == 8
    return jax.shard_map(
        local_fused if planes else local,
        mesh=mesh,
        in_specs=(
            P(AXES, None),
            P(AXES, None),
            P(AXES),
            P(None, "px", "pz"),
        ),
        out_specs=P(AXES, None),
        check_vma=False,
    )
```

```python
import functools
import math

import jax
import jax.numpy as jnp
import numpy as np
from jax import lax
from jax.experimental import pallas as pl
from jax.experimental.pallas import tpu as pltpu
from jax.sharding import PartitionSpec as P

CXP = 8
CYP = 4
NZP = 1024
AXES = ("px", "pz")


def split_table(table):
    high = table.astype(np.float32).astype(jnp.bfloat16)
    low = (table - high.astype(np.float64)).astype(np.float32).astype(jnp.bfloat16)
    return np.asarray(high), np.asarray(low)


def long_table():
    n = np.arange(NZP)[:, None]
    k = np.arange(2 * NZP)[None, :]
    angle = (n * k % (2 * NZP)) * (2.0 * math.pi / (2 * NZP))
    return np.cos(angle) + np.sin(angle)


def short_tables(wide, frequencies):
    period = 2 * wide
    folded = np.minimum(frequencies, period - frequencies)
    angle = (frequencies[:, None] * np.arange(wide)[None, :] % period) * (2.0 * math.pi / period)
    table = np.concatenate((np.cos(angle), np.sin(angle)), axis=0)
    weight = np.where((folded == 0) | (folded == wide), 1.0, 2.0) / period
    count = np.array([(folded == f).sum() for f in folded])
    weight = np.tile(weight / count, 2)
    return table, table * weight[:, None]


def split(values):
    high = lax.reduce_precision(values, 8, 7)
    return high.astype(jnp.bfloat16), (values - high).astype(jnp.bfloat16)


def product(form, values, table):
    high, low = split(values)
    t_high, t_low = table
    dot = lambda a, b: jnp.einsum(form, a, b, preferred_element_type=jnp.float32)
    return dot(high, t_high) + (dot(low, t_high) + dot(high, t_low))


def pick(form, one_hot, values):
    high, low = split(values)
    dot = lambda b: jnp.einsum(form, one_hot, b, preferred_element_type=jnp.float32)
    return dot(high) + dot(low)


def kept_frequencies(wide_y, n_px):
    own = 2 * wide_y // n_px
    return (np.arange(n_px)[:, None] * own + np.arange(own // 2 + 1)[None, :]).reshape(-1)


def local(charge, dest, local_ids, green_hat):
    n_px = lax.axis_size("px")
    n_pz = lax.axis_size("pz")
    n_dev = n_px * n_pz
    wide_x, wide_y = CXP * n_px, CYP * n_pz
    slots = charge.shape[0]
    cap = 2 * slots // n_dev
    pencil_blocks = CXP * CYP * NZP // 128
    own = 2 * wide_y // n_px
    group = 2 * NZP // n_dev

    green = lax.all_to_all(
        green_hat[: wide_x + 1, : own // 2 + 1], "px", split_axis=2, concat_axis=1, tiled=True
    )

    route = dest[:, 0]
    named = (route[:, None] == jnp.arange(n_dev)[None, :]).astype(jnp.bfloat16)
    before = jnp.asarray(np.tril(np.ones((slots, slots)), -1), jnp.bfloat16)
    rank = jnp.sum(
        jnp.einsum("st,td->sd", before, named, preferred_element_type=jnp.float32) * named, axis=1
    ).astype(jnp.int32)
    place = route * cap + rank
    packing = (place[:, None] == jnp.arange(n_dev * cap)[None, :]).astype(jnp.bfloat16)
    sent = pick("sr,sl->rl", packing, charge).reshape(n_dev, cap, 128)
    ids = jnp.einsum(
        "sr,s->r", packing, (local_ids + 1).astype(jnp.bfloat16), preferred_element_type=jnp.float32
    ).reshape(n_dev, 1, cap)
    sent = jnp.concatenate((sent, jnp.pad(ids, ((0, 0), (0, 0), (0, 128 - cap)))), axis=1)
    got = lax.all_to_all(sent, AXES, split_axis=0, concat_axis=0, tiled=True)
    ids = got[:, cap, :cap].reshape(n_dev * cap).astype(jnp.int32) - 1
    placing = (ids[:, None] == jnp.arange(pencil_blocks)[None, :]).astype(jnp.bfloat16)
    field = pick("rb,rl->bl", placing, got[:, :cap].reshape(n_dev * cap, 128))
    field = field.reshape(CXP * CYP, NZP)

    long = split_table(long_table())
    spectrum = product("pz,zk->pk", field, long)
    spectrum = spectrum.reshape(CXP * CYP, n_pz, n_px, group).transpose(2, 1, 0, 3)
    spectrum = spectrum.reshape(n_dev, CXP * CYP, group)
    turned = lax.all_to_all(spectrum, AXES, split_axis=0, concat_axis=0, tiled=True)
    planes = turned.reshape(n_px, n_pz, CXP, CYP, group).transpose(0, 2, 1, 3, 4)
    planes = planes.reshape(wide_x, wide_y, group)

    kept_y = kept_frequencies(wide_y, n_px)
    y_table, y_back = short_tables(wide_y, kept_y)
    x_table, x_back = short_tables(wide_x, np.arange(wide_x + 1))
    planes = product("xyk,qy->xqk", planes, split_table(y_table))
    planes = product("xqk,ux->uqk", planes, split_table(x_table))
    count_x, count_y = wide_x + 1, len(kept_y)
    planes = planes.reshape(2, count_x, 2, count_y, group) * green[None, :, None]
    planes = planes.reshape(2 * count_x, 2 * count_y, group)
    planes = product("uqk,ux->xqk", planes, split_table(x_back))
    planes = product("xqk,qy->xyk", planes, split_table(y_back))

    planes = planes.reshape(n_px, CXP, n_pz, CYP, group).transpose(0, 2, 1, 3, 4)
    planes = planes.reshape(n_dev, CXP * CYP, group)
    turned = lax.all_to_all(planes, AXES, split_axis=0, concat_axis=0, tiled=True)
    spectrum = turned.reshape(n_px, n_pz, CXP * CYP, group).transpose(2, 1, 0, 3)
    spectrum = spectrum.reshape(CXP * CYP, 2 * NZP)
    phi = product("pk,zk->pz", spectrum, long) * (1.0 / (2 * NZP))
    back = pick("rb,bl->rl", placing, phi.reshape(pencil_blocks, 128)).reshape(n_dev, cap, 128)
    got = lax.all_to_all(back, AXES, split_axis=0, concat_axis=0, tiled=True)
    return pick("sr,rl->sl", packing, got.reshape(n_dev * cap, 128))


LANES = 128
GROUP = 64
KEPT = 8
HALF = 32
WIDE = 32
MESH = pl.DeviceIdType.MESH


def unit_rows(frequencies, is_sine, wide):
    period = 2 * wide
    angle = (frequencies[:, None] * np.arange(wide)[None, :] % period) * (2.0 * math.pi / period)
    weight = np.where((frequencies == 0) | (frequencies == wide), 1.0, 2.0) / period
    return np.where(is_sine[:, None], np.sin(angle), np.cos(angle)) * np.sqrt(weight)[:, None]


def folded_table():
    k = np.arange(2 * NZP)[None, :]
    frequency = np.minimum(k, 2 * NZP - k)
    odd = 2 * np.arange(NZP // 2)[:, None] - (NZP - 1)
    angle = (frequency * odd % (4 * NZP)) * (2.0 * math.pi / (4 * NZP))
    weight = np.where((frequency == 0) | (frequency == NZP), 1.0, 2.0) / (2 * NZP)
    return np.where(k < NZP, np.cos(angle), np.sin(angle)) * np.sqrt(weight)


def plane_tables(n_px, n_pz):
    y_tables = []
    for half in range(2):
        raw = half * WIDE + np.arange(HALF)
        folded = np.minimum(raw, 2 * WIDE - raw)
        lone = folded == folded[0]
        frequencies = np.concatenate((folded, np.where(lone, WIDE - folded[0], folded)))
        sine = np.concatenate((np.zeros(HALF, bool), ~lone))
        rows = unit_rows(frequencies, sine, WIDE).reshape(2 * n_px, KEPT, n_pz, CYP)
        table = np.einsum("gqjb,iI,aA->ijabgIqA", rows, np.eye(n_px), np.eye(4))
        y_tables.append(table.reshape(n_px * n_pz * 16, 2 * n_px * n_px * KEPT * 4))
    y_table = np.stack(y_tables)
    base = np.arange(HALF)
    frequencies = np.concatenate((base, np.where(base == 0, WIDE, base)))
    sine = np.concatenate((np.zeros(HALF, bool), base != 0))
    rows = unit_rows(frequencies, sine, WIDE).reshape(2 * HALF, n_px, 2, 4)
    x_table = np.einsum("uiha,qQ->hiqauQ", rows, np.eye(KEPT))
    x_table = x_table.reshape(2 * n_px * KEPT * 4, 2 * HALF * KEPT)
    return y_table, x_table


def halves(values):
    high = values.astype(jnp.bfloat16)
    return high, (values - high.astype(jnp.float32)).astype(jnp.bfloat16)


def mm(a, b, contract=((1,), (0,))):
    return lax.dot_general(a, b, (contract, ((), ())), preferred_element_type=jnp.float32)


def mm_left(values, high, low, contract=((1,), (0,))):
    v_high, v_low = halves(values)
    rows = values.shape[0]
    both = mm(jnp.concatenate((v_high, v_low), axis=0), high, contract)
    return both[:rows] + (both[rows:] + mm(v_high, low, contract))


def mm_pick(one_hot, values):
    high, low = halves(values)
    return mm(one_hot, high) + mm(one_hot, low)


def iota(shape, axis):
    return lax.broadcasted_iota(jnp.int32, shape, axis)


def as_row(column):
    return jnp.transpose(jnp.broadcast_to(column, (column.shape[0], LANES)))[0:1, :]


def as_column(row):
    return jnp.transpose(jnp.broadcast_to(row, (LANES, row.shape[1])))[:, 0:1]


def one(mask):
    return jnp.where(mask, 1.0, 0.0).astype(jnp.bfloat16)


def fused(
    n_px, n_pz, charge_ref, dest_ref, ids_ref, green_hbm, zh_hbm, zl_hbm, yh_hbm, yl_hbm, xh_hbm,
    xl_hbm, out_ref, green, zh, zl, yh, yl, xh, xl, ids_send, ids_recv, charge_send, charge_recv,
    green_send, green_recv, edge_recv, spec_send, spec_recv, back_send, back_recv, out_send, out_recv, scale, folded, taking,
    load_sems, green_sems, send_sems, recv_sems
):
    n_dev = n_px * n_pz
    mi, mj = lax.axis_index("px"), lax.axis_index("pz")
    me = mi * n_pz + mj
    slots = charge_ref.shape[0]
    cap = charge_send.shape[1]
    rows = n_dev * cap
    side = n_dev // 2
    near = me // side
    far = 1 - near
    blocks = CXP * CYP * NZP // LANES

    barrier = pltpu.get_barrier_semaphore()

    def greet(step, carry):
        peer = lax.rem(me + step, n_dev)
        pl.semaphore_signal(
            barrier, inc=1, device_id=(peer // n_pz, lax.rem(peer, n_pz)), device_id_type=MESH
        )
        return carry

    lax.fori_loop(1, n_dev, greet, 0)

    loads = [
        pltpu.make_async_copy(source, target, load_sems.at[number])
        for number, (source, target) in enumerate((
            (green_hbm.at[pl.ds(0, 40)], green), (zh_hbm, zh), (zl_hbm, zl), (yh_hbm.at[near], yh),
            (yl_hbm.at[near], yl), (xh_hbm, xh), (xl_hbm, xl),
        ))
    ]
    for load in loads:
        load.start()

    def block_copy(send, recv, number, peer, part):
        return pltpu.make_async_remote_copy(
            src_ref=send.at[peer],
            dst_ref=recv.at[me],
            send_sem=send_sems.at[number],
            recv_sem=recv_sems.at[number, part],
            device_id=(peer // n_pz, lax.rem(peer, n_pz)),
            device_id_type=MESH,
        )

    def send_far(send, recv, number):
        def body(step, carry):
            block_copy(send, recv, number, far * side + lax.rem(me + step, side), 1).start()
            return carry

        lax.fori_loop(0, side, body, 0)

    def send_near(send, recv, number):
        def body(step, carry):
            block_copy(send, recv, number, near * side + lax.rem(me + step, side), 0).start()
            return carry

        lax.fori_loop(1, side, body, 0)
        recv[me] = send[me]

    def send_all(send, recv, number):
        send_far(send, recv, number)
        send_near(send, recv, number)

    def all_of(send, recv, number, count, part=0):
        return pltpu.make_async_remote_copy(
            src_ref=send.at[pl.ds(0, count)],
            dst_ref=recv.at[pl.ds(0, count)],
            send_sem=send_sems.at[number],
            recv_sem=recv_sems.at[number, part],
            device_id=(mi, mj),
            device_id_type=MESH,
        )

    def wait_near(send, recv, number):
        all_of(send, recv, number, side - 1, 0).wait_recv()

    def wait_far(send, recv, number):
        all_of(send, recv, number, side, 1).wait_recv()

    def wait_both(send, recv, number):
        wait_near(send, recv, number)
        wait_far(send, recv, number)

    dest_row = dest_ref[...].astype(jnp.float32)
    dest = as_column(dest_row)
    named = one(dest == iota((slots, LANES), 1).astype(jnp.float32))
    before = one(iota((slots, slots), 1) < iota((slots, slots), 0))
    rank = jnp.sum(mm(before, named) * named.astype(jnp.float32), axis=1, keepdims=True)
    place = dest * cap + rank
    ids = ids_ref[...].astype(jnp.float32) + 1.0
    owned = jnp.where(dest_row == iota((n_dev, slots), 0).astype(jnp.float32), ids, 0.0)
    ranked = one(rank == iota((slots, LANES), 1).astype(jnp.float32))
    ids_send[...] = mm(owned.astype(jnp.bfloat16), ranked).reshape(n_dev, 1, LANES)
    place_row = as_row(place)

    def pack(half):
        places = (iota((side * cap, 1), 0) + half * (side * cap)).astype(jnp.float32)
        packed = mm_pick(one(place_row == places), charge_ref[...])
        charge_send[pl.ds(half * side, side)] = packed.reshape(side, cap, LANES)

    pack(far)
    pl.semaphore_wait(barrier, n_dev - 1)
    send_all(ids_send, ids_recv, 0)
    send_far(charge_send, charge_recv, 1)
    pack(near)
    send_near(charge_send, charge_recv, 1)

    loads[0].wait()
    wide = [jnp.transpose(green[0:HALF, t * KEPT : (t + 1) * KEPT, :].reshape(HALF * KEPT, 256)) for t in range(2)]
    edge = jnp.concatenate((green[HALF], green[0:40, 0, :], jnp.zeros((LANES - 56, 256), jnp.float32)), axis=0)
    green_send[...] = jnp.concatenate((*wide, jnp.transpose(edge)), axis=1).reshape(n_px, GROUP, 640)
    odd = lax.rem(mi, 2)
    partner = mi + 1 - 2 * odd
    green_copy = pltpu.make_async_remote_copy(
        src_ref=green_send.at[partner],
        dst_ref=green_recv.at[odd],
        send_sem=green_sems.at[0],
        recv_sem=green_sems.at[3],
        device_id=(partner, mj),
        device_id_type=MESH,
    )
    green_copy.start()

    def edge_copy(step):
        target = far * 2 + step
        return pltpu.make_async_remote_copy(
            src_ref=green_send.at[target, :, pl.ds(512, LANES)],
            dst_ref=edge_recv,
            send_sem=green_sems.at[1 + step],
            recv_sem=green_sems.at[4],
            device_id=(target, mj),
            device_id_type=MESH,
        )

    @pl.when(odd == 0)
    def _():
        for step in range(2):
            edge_copy(step).start()

    green_recv[odd] = green_send[mi]

    wait_both(ids_send, ids_recv, 0)
    line = iota((rows, 1), 0)
    cap_bits, line_bits = cap.bit_length() - 1, (CXP * CYP).bit_length() - 1
    from_box = one((line >> cap_bits) == iota((1, n_dev), 1))
    spread = mm(from_box, ids_recv[...].reshape(n_dev, LANES).astype(jnp.bfloat16))
    own_lane = (line & (cap - 1)) == iota((1, LANES), 1)
    ids = jnp.sum(jnp.where(own_lane, spread, 0.0), axis=1, keepdims=True)
    lines = CXP * CYP

    def target_of(index):
        return ((index & (lines - 1)) * (NZP // LANES) + (index >> line_bits) + 1).astype(jnp.float32)

    taking[...] = one(ids == target_of(iota((1, blocks), 1)))
    placing = one(as_row(ids) == target_of(iota((blocks, 1), 0)))
    wait_both(charge_send, charge_recv, 1)
    field = mm_pick(placing, charge_recv[...].reshape(rows, LANES))
    mirror = one(iota((LANES, LANES), 0) + iota((LANES, LANES), 1) == LANES - 1)
    pieces_z = NZP // LANES
    middle = lines * pieces_z // 2
    front = field[:middle]
    m_high, m_low = halves(field[middle:])
    rear = mm(m_high, mirror) + mm(m_low, mirror)
    front = jnp.concatenate([front[lines * c : lines * (c + 1)] for c in range(pieces_z // 2)], axis=1)
    rear = jnp.concatenate(
        [rear[lines * c : lines * (c + 1)] for c in range(pieces_z // 2 - 1, -1, -1)], axis=1
    )

    for odd_part, part in enumerate((front + rear, front - rear)):
        folded[odd_part] = jnp.concatenate(halves(part), axis=0)
    loads[1].wait()
    loads[2].wait()
    first = iota((lines // 2, LANES), 1) < GROUP

    def forward(half, part):
        def body(step, carry):
            two = lax.rem(mj // 2 + step, n_pz // 2)
            columns = pl.ds(pl.multiple_of(half * NZP + two * 256, 256), 256)
            part_of = folded[two // (n_pz // 4)]
            both = mm(part_of, zh[:, columns])
            total = both[:lines] + (both[lines:] + mm(part_of[:lines], zl[:, columns]))
            for t in range(2):
                j = two * 2 + t
                tile = total[:, t * LANES : (t + 1) * LANES]
                low, high = tile[: lines // 2], tile[lines // 2 :]
                low_turned, high_turned = pltpu.roll(low, GROUP, 1), pltpu.roll(high, GROUP, 1)
                at = half * side + j
                spec_send[at] = jnp.where(first, low, high_turned)
                spec_send[at + n_pz] = jnp.where(first, low_turned, high)
                for peer in (at, at + n_pz):
                    if part == 1:
                        block_copy(spec_send, spec_recv, 3, peer, 1).start()
                    else:

                        @pl.when(peer != me)
                        def _():
                            block_copy(spec_send, spec_recv, 3, peer, 0).start()

            return carry

        lax.fori_loop(0, n_pz // 2, body, 0)

    forward(far, 1)
    forward(near, 0)
    spec_recv[me] = spec_send[me]

    green_copy.wait_recv()
    edge_copy(0).wait_recv()
    target = iota((1, 512), 1)
    wanted = jnp.where(target == 256, HALF, (target & 255) >> 3) + 2 * KEPT
    wanted = jnp.where((target & (KEPT - 1)) == 0, wanted, -1)
    picking = one(iota((LANES, 1), 0) == wanted)
    e_high, e_low = halves(edge_recv[...])
    lone = mm(e_high, picking) + mm(e_low, picking)
    lane = iota((GROUP, LANES), 1)
    for parity in range(2):
        edge = green_recv[parity, :, 512:640]
        for t in range(2):
            wide = green_recv[parity, :, t * 256 : (t + 1) * 256]
            turned = edge if t == 0 else pltpu.roll(edge, LANES - KEPT, 1)
            start = jnp.where(lane < KEPT, turned, wide[:, :LANES])
            full = jnp.concatenate((wide, start, wide[:, LANES:]), axis=1)
            at = (2 * parity + t) * GROUP
            scale[at : at + GROUP, :] = full
            if parity == 0 and t == 0:
                full = jnp.where((target & (KEPT - 1)) == 0, lone, full)
            at = at + n_px * GROUP
            scale[at : at + GROUP, :] = full

    for load in loads[3:]:
        load.wait()

    def side_planes(half):
        taken = spec_recv[pl.ds(half * side, side)].reshape(side * 16, LANES)
        table_rows = pl.ds(pl.multiple_of(half * (side * 16), side * 16), side * 16)
        return mm_left(jnp.transpose(taken), yh[table_rows, :], yl[table_rows, :])

    wait_near(spec_send, spec_recv, 3)
    planes = side_planes(near)
    wait_far(spec_send, spec_recv, 3)
    planes = planes + side_planes(far)
    groups = 2 * n_px
    planes = jnp.concatenate(
        [
            jnp.concatenate(
                [planes[h * GROUP : (h + 1) * GROUP, g * LANES : (g + 1) * LANES] for h in range(2)], axis=1
            )
            for g in range(groups)
        ],
        axis=0,
    )
    planes = mm_left(planes, xh[...], xl[...]) * scale[...]
    planes = mm_left(planes, xh[...], xl[...], ((1,), (1,)))
    planes = jnp.concatenate(
        [
            jnp.concatenate(
                [planes[g * GROUP : (g + 1) * GROUP, h * LANES : (h + 1) * LANES] for g in range(groups)], axis=1
            )
            for h in range(2)
        ],
        axis=0,
    )
    p_high, p_low = halves(planes)
    right = ((1,), (1,))

    def row_back(i):
        table_rows = pl.ds(pl.multiple_of(i * (n_pz * 16), n_pz * 16), n_pz * 16)
        high, low = yh[table_rows, :], yl[table_rows, :]
        given = mm(high, p_high, right) + (mm(high, p_low, right) + mm(low, p_high, right))
        back_send[pl.ds(i * n_pz, n_pz)] = given.reshape(n_pz, 16, LANES)

    for turn in range(2):
        line_i = far * 2 + lax.rem(mi + turn, 2)
        row_back(line_i)

        def send_row(step, carry, line_i=line_i):
            block_copy(back_send, back_recv, 4, line_i * n_pz + lax.rem(mj + step, n_pz), 1).start()
            return carry

        lax.fori_loop(0, n_pz, send_row, 0)
    for turn in range(2):
        row_back(near * 2 + turn)
    send_near(back_send, back_recv, 4)

    def side_phi(half):
        pieces = []
        for j in range(n_pz):
            left, other = back_recv[half * side + j], back_recv[half * side + n_pz + j]
            low = jnp.where(first, left, pltpu.roll(other, GROUP, 1))
            high = jnp.where(first, pltpu.roll(left, GROUP, 1), other)
            pieces.append(jnp.concatenate((low, high), axis=0))
        given = []
        for odd_part in range(2):
            columns = pl.ds(pl.multiple_of(half * NZP + odd_part * (NZP // 2), NZP // 2), NZP // 2)
            group = pieces[odd_part * n_pz // 2 : (odd_part + 1) * n_pz // 2]
            given.append(mm_left(jnp.concatenate(group, axis=1), zh[:, columns], zl[:, columns], right))
        return given

    wait_near(back_send, back_recv, 4)
    near_phi = side_phi(near)
    wait_far(back_send, back_recv, 4)
    even, odd_sum = [one_side + other for one_side, other in zip(near_phi, side_phi(far))]
    front, rear = even + odd_sum, even - odd_sum
    front = [front[:, c * LANES : (c + 1) * LANES] for c in range(pieces_z // 2)]
    rear = [rear[:, c * LANES : (c + 1) * LANES] for c in range(pieces_z // 2 - 1, -1, -1)]
    m_high, m_low = halves(jnp.concatenate(rear, axis=0))
    phi = jnp.concatenate((*front, mm(m_high, mirror) + mm(m_low, mirror)), axis=0)
    phi_high, phi_low = halves(phi)

    def take(half):
        one_hot = taking[pl.ds(pl.multiple_of(half * (side * cap), side * cap), side * cap), :]
        taken = mm(one_hot, phi_high) + mm(one_hot, phi_low)
        out_send[pl.ds(half * side, side)] = taken.reshape(side, cap, LANES)

    take(far)
    send_far(out_send, out_recv, 5)
    take(near)
    send_near(out_send, out_recv, 5)
    unpacking = one(place == iota((slots, rows), 1).astype(jnp.float32))
    wait_both(out_send, out_recv, 5)
    out_ref[...] = mm_pick(unpacking, out_recv[...].reshape(rows, LANES))

    all_of(ids_send, ids_recv, 0, n_dev - 1).wait_send()
    all_of(charge_send, charge_recv, 1, n_dev - 1).wait_send()
    green_copy.wait_send()

    @pl.when(odd == 0)
    def _():
        for step in range(2):
            edge_copy(step).wait_send()

    all_of(spec_send, spec_recv, 3, n_dev - 1).wait_send()
    all_of(back_send, back_recv, 4, n_dev - 1).wait_send()
    all_of(out_send, out_recv, 5, n_dev - 1).wait_send()


def local_fused(charge, dest, local_ids, green_hat):
    n_px, n_pz = lax.axis_size("px"), lax.axis_size("pz")
    n_dev = n_px * n_pz
    slots = charge.shape[0]
    cap = 2 * slots // n_dev
    y_table, x_table = plane_tables(n_px, n_pz)
    z_table = folded_table().reshape(NZP // 2, n_pz, 2, 2 * GROUP).transpose(0, 2, 1, 3)
    z_table = z_table.reshape(NZP // 2, 2 * NZP)
    tables = [
        piece
        for table in (z_table, y_table, x_table)
        for piece in split_table(table)
    ]
    exchange = lambda lead, rows: [pltpu.VMEM((lead, rows, LANES), jnp.float32)] * 2
    vmem, anywhere = pl.BlockSpec(memory_space=pltpu.VMEM), pl.BlockSpec(memory_space=pltpu.HBM)
    return pl.pallas_call(
        functools.partial(fused, n_px, n_pz),
        out_shape=jax.ShapeDtypeStruct(charge.shape, jnp.float32),
        in_specs=[vmem] * 3 + [anywhere] * 7,
        out_specs=vmem,
        scratch_shapes=[
            pltpu.VMEM((40,) + green_hat.shape[1:], jnp.float32),
            *[pltpu.VMEM(table.shape[-2:], jnp.bfloat16) for table in tables],
            *exchange(n_dev, 1),
            *exchange(n_dev, cap),
            pltpu.VMEM((n_px, GROUP, 640), jnp.float32),
            pltpu.VMEM((2, GROUP, 640), jnp.float32),
            pltpu.VMEM((GROUP, LANES), jnp.float32),
            *exchange(n_dev, 16),
            *exchange(n_dev, 16),
            *exchange(n_dev, cap),
            pltpu.VMEM((2 * n_px * GROUP, 2 * HALF * KEPT), jnp.float32),
            pltpu.VMEM((2, 2 * CXP * CYP, NZP // 2), jnp.bfloat16),
            pltpu.VMEM((n_dev * cap, CXP * CYP * NZP // LANES), jnp.bfloat16),
            pltpu.SemaphoreType.DMA((7,)),
            pltpu.SemaphoreType.DMA((5,)),
            pltpu.SemaphoreType.DMA((6,)),
            pltpu.SemaphoreType.DMA((6, 2)),
        ],
        compiler_params=pltpu.CompilerParams(
            collective_id=0, has_side_effects=True, vmem_limit_bytes=64 * 1024 * 1024
        ),
    )(charge, dest.reshape(1, slots), local_ids.reshape(1, slots), green_hat, *tables)


def solution(mesh):
    planes = mesh.shape["px"] == 4 and mesh.shape["pz"] == 8
    return jax.shard_map(
        local_fused if planes else local,
        mesh=mesh,
        in_specs=(
            P(AXES, None),
            P(AXES, None),
            P(AXES),
            P(None, "px", "pz"),
        ),
        out_specs=P(AXES, None),
        check_vma=False,
    )
```

```python
import functools
import math

import jax
import jax.numpy as jnp
import numpy as np
from jax import lax
from jax.experimental import pallas as pl
from jax.experimental.pallas import tpu as pltpu
from jax.sharding import PartitionSpec as P

CXP = 8
CYP = 4
NZP = 1024
AXES = ("px", "pz")


def split_table(table):
    high = table.astype(np.float32).astype(jnp.bfloat16)
    low = (table - high.astype(np.float64)).astype(np.float32).astype(jnp.bfloat16)
    return np.asarray(high), np.asarray(low)


def long_table():
    n = np.arange(NZP)[:, None]
    k = np.arange(2 * NZP)[None, :]
    angle = (n * k % (2 * NZP)) * (2.0 * math.pi / (2 * NZP))
    return np.cos(angle) + np.sin(angle)


def short_tables(wide, frequencies):
    period = 2 * wide
    folded = np.minimum(frequencies, period - frequencies)
    angle = (frequencies[:, None] * np.arange(wide)[None, :] % period) * (2.0 * math.pi / period)
    table = np.concatenate((np.cos(angle), np.sin(angle)), axis=0)
    weight = np.where((folded == 0) | (folded == wide), 1.0, 2.0) / period
    count = np.array([(folded == f).sum() for f in folded])
    weight = np.tile(weight / count, 2)
    return table, table * weight[:, None]


def split(values):
    high = lax.reduce_precision(values, 8, 7)
    return high.astype(jnp.bfloat16), (values - high).astype(jnp.bfloat16)


def product(form, values, table):
    high, low = split(values)
    t_high, t_low = table
    dot = lambda a, b: jnp.einsum(form, a, b, preferred_element_type=jnp.float32)
    return dot(high, t_high) + (dot(low, t_high) + dot(high, t_low))


def pick(form, one_hot, values):
    high, low = split(values)
    dot = lambda b: jnp.einsum(form, one_hot, b, preferred_element_type=jnp.float32)
    return dot(high) + dot(low)


def kept_frequencies(wide_y, n_px):
    own = 2 * wide_y // n_px
    return (np.arange(n_px)[:, None] * own + np.arange(own // 2 + 1)[None, :]).reshape(-1)


def local(charge, dest, local_ids, green_hat):
    n_px = lax.axis_size("px")
    n_pz = lax.axis_size("pz")
    n_dev = n_px * n_pz
    wide_x, wide_y = CXP * n_px, CYP * n_pz
    slots = charge.shape[0]
    cap = 2 * slots // n_dev
    pencil_blocks = CXP * CYP * NZP // 128
    own = 2 * wide_y // n_px
    group = 2 * NZP // n_dev

    green = lax.all_to_all(
        green_hat[: wide_x + 1, : own // 2 + 1], "px", split_axis=2, concat_axis=1, tiled=True
    )

    route = dest[:, 0]
    named = (route[:, None] == jnp.arange(n_dev)[None, :]).astype(jnp.bfloat16)
    before = jnp.asarray(np.tril(np.ones((slots, slots)), -1), jnp.bfloat16)
    rank = jnp.sum(
        jnp.einsum("st,td->sd", before, named, preferred_element_type=jnp.float32) * named, axis=1
    ).astype(jnp.int32)
    place = route * cap + rank
    packing = (place[:, None] == jnp.arange(n_dev * cap)[None, :]).astype(jnp.bfloat16)
    sent = pick("sr,sl->rl", packing, charge).reshape(n_dev, cap, 128)
    ids = jnp.einsum(
        "sr,s->r", packing, (local_ids + 1).astype(jnp.bfloat16), preferred_element_type=jnp.float32
    ).reshape(n_dev, 1, cap)
    sent = jnp.concatenate((sent, jnp.pad(ids, ((0, 0), (0, 0), (0, 128 - cap)))), axis=1)
    got = lax.all_to_all(sent, AXES, split_axis=0, concat_axis=0, tiled=True)
    ids = got[:, cap, :cap].reshape(n_dev * cap).astype(jnp.int32) - 1
    placing = (ids[:, None] == jnp.arange(pencil_blocks)[None, :]).astype(jnp.bfloat16)
    field = pick("rb,rl->bl", placing, got[:, :cap].reshape(n_dev * cap, 128))
    field = field.reshape(CXP * CYP, NZP)

    long = split_table(long_table())
    spectrum = product("pz,zk->pk", field, long)
    spectrum = spectrum.reshape(CXP * CYP, n_pz, n_px, group).transpose(2, 1, 0, 3)
    spectrum = spectrum.reshape(n_dev, CXP * CYP, group)
    turned = lax.all_to_all(spectrum, AXES, split_axis=0, concat_axis=0, tiled=True)
    planes = turned.reshape(n_px, n_pz, CXP, CYP, group).transpose(0, 2, 1, 3, 4)
    planes = planes.reshape(wide_x, wide_y, group)

    kept_y = kept_frequencies(wide_y, n_px)
    y_table, y_back = short_tables(wide_y, kept_y)
    x_table, x_back = short_tables(wide_x, np.arange(wide_x + 1))
    planes = product("xyk,qy->xqk", planes, split_table(y_table))
    planes = product("xqk,ux->uqk", planes, split_table(x_table))
    count_x, count_y = wide_x + 1, len(kept_y)
    planes = planes.reshape(2, count_x, 2, count_y, group) * green[None, :, None]
    planes = planes.reshape(2 * count_x, 2 * count_y, group)
    planes = product("uqk,ux->xqk", planes, split_table(x_back))
    planes = product("xqk,qy->xyk", planes, split_table(y_back))

    planes = planes.reshape(n_px, CXP, n_pz, CYP, group).transpose(0, 2, 1, 3, 4)
    planes = planes.reshape(n_dev, CXP * CYP, group)
    turned = lax.all_to_all(planes, AXES, split_axis=0, concat_axis=0, tiled=True)
    spectrum = turned.reshape(n_px, n_pz, CXP * CYP, group).transpose(2, 1, 0, 3)
    spectrum = spectrum.reshape(CXP * CYP, 2 * NZP)
    phi = product("pk,zk->pz", spectrum, long) * (1.0 / (2 * NZP))
    back = pick("rb,bl->rl", placing, phi.reshape(pencil_blocks, 128)).reshape(n_dev, cap, 128)
    got = lax.all_to_all(back, AXES, split_axis=0, concat_axis=0, tiled=True)
    return pick("sr,rl->sl", packing, got.reshape(n_dev * cap, 128))


LANES = 128
GROUP = 64
KEPT = 8
HALF = 32
WIDE = 32
MESH = pl.DeviceIdType.MESH


def unit_rows(frequencies, is_sine, wide):
    period = 2 * wide
    angle = (frequencies[:, None] * np.arange(wide)[None, :] % period) * (2.0 * math.pi / period)
    weight = np.where((frequencies == 0) | (frequencies == wide), 1.0, 2.0) / period
    return np.where(is_sine[:, None], np.sin(angle), np.cos(angle)) * np.sqrt(weight)[:, None]


def folded_table():
    k = np.arange(2 * NZP)[None, :]
    frequency = np.minimum(k, 2 * NZP - k)
    odd = 2 * np.arange(NZP // 2)[:, None] - (NZP - 1)
    angle = (frequency * odd % (4 * NZP)) * (2.0 * math.pi / (4 * NZP))
    weight = np.where((frequency == 0) | (frequency == NZP), 1.0, 2.0) / (2 * NZP)
    return np.where(k < NZP, np.cos(angle), np.sin(angle)) * np.sqrt(weight)


def plane_tables(n_px, n_pz):
    y_tables = []
    for half in range(2):
        raw = half * WIDE + np.arange(HALF)
        folded = np.minimum(raw, 2 * WIDE - raw)
        lone = folded == folded[0]
        frequencies = np.concatenate((folded, np.where(lone, WIDE - folded[0], folded)))
        sine = np.concatenate((np.zeros(HALF, bool), ~lone))
        rows = unit_rows(frequencies, sine, WIDE).reshape(2 * n_px, KEPT, n_pz, CYP)
        table = np.einsum("gqjb,iI,aA->ijabgIqA", rows, np.eye(n_px), np.eye(4))
        y_tables.append(table.reshape(n_px * n_pz * 16, 2 * n_px * n_px * KEPT * 4))
    y_table = np.stack(y_tables)
    base = np.arange(HALF)
    frequencies = np.concatenate((base, np.where(base == 0, WIDE, base)))
    sine = np.concatenate((np.zeros(HALF, bool), base != 0))
    rows = unit_rows(frequencies, sine, WIDE).reshape(2 * HALF, n_px, 2, 4)
    x_table = np.einsum("uiha,qQ->hiqauQ", rows, np.eye(KEPT))
    x_table = x_table.reshape(2 * n_px * KEPT * 4, 2 * HALF * KEPT)
    return y_table, x_table


def halves(values):
    high = values.astype(jnp.bfloat16)
    return high, (values - high.astype(jnp.float32)).astype(jnp.bfloat16)


def mm(a, b, contract=((1,), (0,))):
    return lax.dot_general(a, b, (contract, ((), ())), preferred_element_type=jnp.float32)


def mm_left(values, high, low, contract=((1,), (0,))):
    v_high, v_low = halves(values)
    rows = values.shape[0]
    both = mm(jnp.concatenate((v_high, v_low), axis=0), high, contract)
    return both[:rows] + (both[rows:] + mm(v_high, low, contract))


def mm_pick(one_hot, values):
    high, low = halves(values)
    return mm(one_hot, high) + mm(one_hot, low)


def iota(shape, axis):
    return lax.broadcasted_iota(jnp.int32, shape, axis)


def as_row(column):
    return jnp.transpose(jnp.broadcast_to(column, (column.shape[0], LANES)))[0:1, :]


def as_column(row):
    return jnp.transpose(jnp.broadcast_to(row, (LANES, row.shape[1])))[:, 0:1]


def one(mask):
    return jnp.where(mask, 1.0, 0.0).astype(jnp.bfloat16)


def fused(
    n_px, n_pz, charge_ref, dest_ref, ids_ref, green_hbm, zh_hbm, zl_hbm, yh_hbm, yl_hbm, xh_hbm,
    xl_hbm, out_ref, green, zh, zl, yh, yl, xh, xl, ids_send, ids_recv, charge_send, charge_recv,
    green_send, green_recv, edge_recv, spec_send, spec_recv, back_send, back_recv, out_send, out_recv, scale, folded, taking,
    load_sems, green_sems, send_sems, recv_sems
):
    n_dev = n_px * n_pz
    mi, mj = lax.axis_index("px"), lax.axis_index("pz")
    me = mi * n_pz + mj
    slots = charge_ref.shape[0]
    cap = charge_send.shape[1]
    rows = n_dev * cap
    side = n_dev // 2
    near = me // side
    far = 1 - near
    blocks = CXP * CYP * NZP // LANES

    barrier = pltpu.get_barrier_semaphore()

    def greet(step, carry):
        peer = lax.rem(me + step, n_dev)
        pl.semaphore_signal(
            barrier, inc=1, device_id=(peer // n_pz, lax.rem(peer, n_pz)), device_id_type=MESH
        )
        return carry

    lax.fori_loop(1, n_dev, greet, 0)

    loads = [
        pltpu.make_async_copy(source, target, load_sems.at[number])
        for number, (source, target) in enumerate((
            (green_hbm.at[pl.ds(0, 40)], green), (zh_hbm, zh), (zl_hbm, zl), (yh_hbm.at[near], yh),
            (yl_hbm.at[near], yl), (xh_hbm, xh), (xl_hbm, xl),
        ))
    ]
    for load in loads:
        load.start()

    def block_copy(send, recv, number, peer, part):
        return pltpu.make_async_remote_copy(
            src_ref=send.at[peer],
            dst_ref=recv.at[me],
            send_sem=send_sems.at[number],
            recv_sem=recv_sems.at[number, part],
            device_id=(peer // n_pz, lax.rem(peer, n_pz)),
            device_id_type=MESH,
        )

    def send_far(send, recv, number):
        for step in range(side):
            block_copy(send, recv, number, far * side + lax.rem(me + step, side), 1).start()

    def send_near(send, recv, number):
        for step in range(1, side):
            block_copy(send, recv, number, near * side + lax.rem(me + step, side), 0).start()
        recv[me] = send[me]

    def send_all(send, recv, number):
        send_far(send, recv, number)
        send_near(send, recv, number)

    def all_of(send, recv, number, count, part=0):
        return pltpu.make_async_remote_copy(
            src_ref=send.at[pl.ds(0, count)],
            dst_ref=recv.at[pl.ds(0, count)],
            send_sem=send_sems.at[number],
            recv_sem=recv_sems.at[number, part],
            device_id=(mi, mj),
            device_id_type=MESH,
        )

    def wait_near(send, recv, number):
        all_of(send, recv, number, side - 1, 0).wait_recv()

    def wait_far(send, recv, number):
        all_of(send, recv, number, side, 1).wait_recv()

    def wait_both(send, recv, number):
        wait_near(send, recv, number)
        wait_far(send, recv, number)

    dest_row = dest_ref[...].astype(jnp.float32)
    dest = as_column(dest_row)
    named = one(dest == iota((slots, LANES), 1).astype(jnp.float32))
    before = one(iota((slots, slots), 1) < iota((slots, slots), 0))
    rank = jnp.sum(mm(before, named) * named.astype(jnp.float32), axis=1, keepdims=True)
    place = dest * cap + rank
    ids = ids_ref[...].astype(jnp.float32) + 1.0
    owned = jnp.where(dest_row == iota((n_dev, slots), 0).astype(jnp.float32), ids, 0.0)
    ranked = one(rank == iota((slots, LANES), 1).astype(jnp.float32))
    ids_send[...] = mm(owned.astype(jnp.bfloat16), ranked).reshape(n_dev, 1, LANES)
    place_row = as_row(place)

    def pack(half):
        places = (iota((side * cap, 1), 0) + half * (side * cap)).astype(jnp.float32)
        packed = mm_pick(one(place_row == places), charge_ref[...])
        charge_send[pl.ds(half * side, side)] = packed.reshape(side, cap, LANES)

    pack(far)
    pl.semaphore_wait(barrier, n_dev - 1)
    send_all(ids_send, ids_recv, 0)
    send_far(charge_send, charge_recv, 1)
    pack(near)
    send_near(charge_send, charge_recv, 1)

    loads[0].wait()
    wide = [jnp.transpose(green[0:HALF, t * KEPT : (t + 1) * KEPT, :].reshape(HALF * KEPT, 256)) for t in range(2)]
    edge = jnp.concatenate((green[HALF], green[0:40, 0, :], jnp.zeros((LANES - 56, 256), jnp.float32)), axis=0)
    green_send[...] = jnp.concatenate((*wide, jnp.transpose(edge)), axis=1).reshape(n_px, GROUP, 640)
    odd = lax.rem(mi, 2)
    partner = mi + 1 - 2 * odd
    green_copy = pltpu.make_async_remote_copy(
        src_ref=green_send.at[partner],
        dst_ref=green_recv.at[odd],
        send_sem=green_sems.at[0],
        recv_sem=green_sems.at[3],
        device_id=(partner, mj),
        device_id_type=MESH,
    )
    green_copy.start()

    def edge_copy(step):
        target = far * 2 + step
        return pltpu.make_async_remote_copy(
            src_ref=green_send.at[target, :, pl.ds(512, LANES)],
            dst_ref=edge_recv,
            send_sem=green_sems.at[1 + step],
            recv_sem=green_sems.at[4],
            device_id=(target, mj),
            device_id_type=MESH,
        )

    @pl.when(odd == 0)
    def _():
        for step in range(2):
            edge_copy(step).start()

    green_recv[odd] = green_send[mi]

    wait_both(ids_send, ids_recv, 0)
    line = iota((rows, 1), 0)
    cap_bits, line_bits = cap.bit_length() - 1, (CXP * CYP).bit_length() - 1
    from_box = one((line >> cap_bits) == iota((1, n_dev), 1))
    spread = mm(from_box, ids_recv[...].reshape(n_dev, LANES).astype(jnp.bfloat16))
    own_lane = (line & (cap - 1)) == iota((1, LANES), 1)
    ids = jnp.sum(jnp.where(own_lane, spread, 0.0), axis=1, keepdims=True)
    lines = CXP * CYP

    def target_of(index):
        return ((index & (lines - 1)) * (NZP // LANES) + (index >> line_bits) + 1).astype(jnp.float32)

    taking[...] = one(ids == target_of(iota((1, blocks), 1)))
    placing = one(as_row(ids) == target_of(iota((blocks, 1), 0)))
    wait_both(charge_send, charge_recv, 1)
    field = mm_pick(placing, charge_recv[...].reshape(rows, LANES))
    mirror = one(iota((LANES, LANES), 0) + iota((LANES, LANES), 1) == LANES - 1)
    pieces_z = NZP // LANES
    middle = lines * pieces_z // 2
    front = field[:middle]
    m_high, m_low = halves(field[middle:])
    rear = mm(m_high, mirror) + mm(m_low, mirror)
    front = jnp.concatenate([front[lines * c : lines * (c + 1)] for c in range(pieces_z // 2)], axis=1)
    rear = jnp.concatenate(
        [rear[lines * c : lines * (c + 1)] for c in range(pieces_z // 2 - 1, -1, -1)], axis=1
    )

    for odd_part, part in enumerate((front + rear, front - rear)):
        folded[odd_part] = jnp.concatenate(halves(part), axis=0)
    loads[1].wait()
    loads[2].wait()
    first = iota((lines // 2, LANES), 1) < GROUP

    def forward(half, part):
        def body(step, carry):
            two = lax.rem(mj // 2 + step, n_pz // 2)
            columns = pl.ds(pl.multiple_of(half * NZP + two * 256, 256), 256)
            part_of = folded[two // (n_pz // 4)]
            both = mm(part_of, zh[:, columns])
            total = both[:lines] + (both[lines:] + mm(part_of[:lines], zl[:, columns]))
            for t in range(2):
                j = two * 2 + t
                tile = total[:, t * LANES : (t + 1) * LANES]
                low, high = tile[: lines // 2], tile[lines // 2 :]
                low_turned, high_turned = pltpu.roll(low, GROUP, 1), pltpu.roll(high, GROUP, 1)
                at = half * side + j
                spec_send[at] = jnp.where(first, low, high_turned)
                spec_send[at + n_pz] = jnp.where(first, low_turned, high)
                for peer in (at, at + n_pz):
                    if part == 1:
                        block_copy(spec_send, spec_recv, 3, peer, 1).start()
                    else:

                        @pl.when(peer != me)
                        def _():
                            block_copy(spec_send, spec_recv, 3, peer, 0).start()

            return carry

        lax.fori_loop(0, n_pz // 2, body, 0)

    forward(far, 1)
    forward(near, 0)
    spec_recv[me] = spec_send[me]

    green_copy.wait_recv()
    edge_copy(0).wait_recv()
    target = iota((1, 512), 1)
    wanted = jnp.where(target == 256, HALF, (target & 255) >> 3) + 2 * KEPT
    wanted = jnp.where((target & (KEPT - 1)) == 0, wanted, -1)
    picking = one(iota((LANES, 1), 0) == wanted)
    e_high, e_low = halves(edge_recv[...])
    lone = mm(e_high, picking) + mm(e_low, picking)
    lane = iota((GROUP, LANES), 1)
    for parity in range(2):
        edge = green_recv[parity, :, 512:640]
        for t in range(2):
            wide = green_recv[parity, :, t * 256 : (t + 1) * 256]
            turned = edge if t == 0 else pltpu.roll(edge, LANES - KEPT, 1)
            start = jnp.where(lane < KEPT, turned, wide[:, :LANES])
            full = jnp.concatenate((wide, start, wide[:, LANES:]), axis=1)
            at = (2 * parity + t) * GROUP
            scale[at : at + GROUP, :] = full
            if parity == 0 and t == 0:
                full = jnp.where((target & (KEPT - 1)) == 0, lone, full)
            at = at + n_px * GROUP
            scale[at : at + GROUP, :] = full

    for load in loads[3:]:
        load.wait()

    def side_planes(half):
        taken = spec_recv[pl.ds(half * side, side)].reshape(side * 16, LANES)
        table_rows = pl.ds(pl.multiple_of(half * (side * 16), side * 16), side * 16)
        return mm_left(jnp.transpose(taken), yh[table_rows, :], yl[table_rows, :])

    wait_near(spec_send, spec_recv, 3)
    planes = side_planes(near)
    wait_far(spec_send, spec_recv, 3)
    planes = planes + side_planes(far)
    groups = 2 * n_px
    planes = jnp.concatenate(
        [
            jnp.concatenate(
                [planes[h * GROUP : (h + 1) * GROUP, g * LANES : (g + 1) * LANES] for h in range(2)], axis=1
            )
            for g in range(groups)
        ],
        axis=0,
    )
    planes = mm_left(planes, xh[...], xl[...]) * scale[...]
    planes = mm_left(planes, xh[...], xl[...], ((1,), (1,)))
    planes = jnp.concatenate(
        [
            jnp.concatenate(
                [planes[g * GROUP : (g + 1) * GROUP, h * LANES : (h + 1) * LANES] for g in range(groups)], axis=1
            )
            for h in range(2)
        ],
        axis=0,
    )
    p_high, p_low = halves(planes)
    right = ((1,), (1,))

    def row_back(i):
        table_rows = pl.ds(pl.multiple_of(i * (n_pz * 16), n_pz * 16), n_pz * 16)
        high, low = yh[table_rows, :], yl[table_rows, :]
        given = mm(high, p_high, right) + (mm(high, p_low, right) + mm(low, p_high, right))
        back_send[pl.ds(i * n_pz, n_pz)] = given.reshape(n_pz, 16, LANES)

    for turn in range(2):
        line_i = far * 2 + lax.rem(mi + turn, 2)
        row_back(line_i)
        for step in range(n_pz):
            block_copy(back_send, back_recv, 4, line_i * n_pz + lax.rem(mj + step, n_pz), 1).start()
    for turn in range(2):
        row_back(near * 2 + turn)
    send_near(back_send, back_recv, 4)

    def side_phi(half):
        pieces = []
        for j in range(n_pz):
            left, other = back_recv[half * side + j], back_recv[half * side + n_pz + j]
            low = jnp.where(first, left, pltpu.roll(other, GROUP, 1))
            high = jnp.where(first, pltpu.roll(left, GROUP, 1), other)
            pieces.append(jnp.concatenate((low, high), axis=0))
        given = []
        for odd_part in range(2):
            columns = pl.ds(pl.multiple_of(half * NZP + odd_part * (NZP // 2), NZP // 2), NZP // 2)
            group = pieces[odd_part * n_pz // 2 : (odd_part + 1) * n_pz // 2]
            given.append(mm_left(jnp.concatenate(group, axis=1), zh[:, columns], zl[:, columns], right))
        return given

    wait_near(back_send, back_recv, 4)
    near_phi = side_phi(near)
    wait_far(back_send, back_recv, 4)
    even, odd_sum = [one_side + other for one_side, other in zip(near_phi, side_phi(far))]
    front, rear = even + odd_sum, even - odd_sum
    front = [front[:, c * LANES : (c + 1) * LANES] for c in range(pieces_z // 2)]
    rear = [rear[:, c * LANES : (c + 1) * LANES] for c in range(pieces_z // 2 - 1, -1, -1)]
    m_high, m_low = halves(jnp.concatenate(rear, axis=0))
    phi = jnp.concatenate((*front, mm(m_high, mirror) + mm(m_low, mirror)), axis=0)
    phi_high, phi_low = halves(phi)

    def take(half):
        one_hot = taking[pl.ds(pl.multiple_of(half * (side * cap), side * cap), side * cap), :]
        taken = mm(one_hot, phi_high) + mm(one_hot, phi_low)
        out_send[pl.ds(half * side, side)] = taken.reshape(side, cap, LANES)

    take(far)
    send_far(out_send, out_recv, 5)
    take(near)
    send_near(out_send, out_recv, 5)
    unpacking = one(place == iota((slots, rows), 1).astype(jnp.float32))
    wait_both(out_send, out_recv, 5)
    out_ref[...] = mm_pick(unpacking, out_recv[...].reshape(rows, LANES))

    all_of(ids_send, ids_recv, 0, n_dev - 1).wait_send()
    all_of(charge_send, charge_recv, 1, n_dev - 1).wait_send()
    green_copy.wait_send()

    @pl.when(odd == 0)
    def _():
        for step in range(2):
            edge_copy(step).wait_send()

    all_of(spec_send, spec_recv, 3, n_dev - 1).wait_send()
    all_of(back_send, back_recv, 4, n_dev - 1).wait_send()
    all_of(out_send, out_recv, 5, n_dev - 1).wait_send()


def local_fused(charge, dest, local_ids, green_hat):
    n_px, n_pz = lax.axis_size("px"), lax.axis_size("pz")
    n_dev = n_px * n_pz
    slots = charge.shape[0]
    cap = 2 * slots // n_dev
    y_table, x_table = plane_tables(n_px, n_pz)
    z_table = folded_table().reshape(NZP // 2, n_pz, 2, 2 * GROUP).transpose(0, 2, 1, 3)
    z_table = z_table.reshape(NZP // 2, 2 * NZP)
    tables = [
        piece
        for table in (z_table, y_table, x_table)
        for piece in split_table(table)
    ]
    exchange = lambda lead, rows: [pltpu.VMEM((lead, rows, LANES), jnp.float32)] * 2
    vmem, anywhere = pl.BlockSpec(memory_space=pltpu.VMEM), pl.BlockSpec(memory_space=pltpu.HBM)
    return pl.pallas_call(
        functools.partial(fused, n_px, n_pz),
        out_shape=jax.ShapeDtypeStruct(charge.shape, jnp.float32),
        in_specs=[vmem] * 3 + [anywhere] * 7,
        out_specs=vmem,
        scratch_shapes=[
            pltpu.VMEM((40,) + green_hat.shape[1:], jnp.float32),
            *[pltpu.VMEM(table.shape[-2:], jnp.bfloat16) for table in tables],
            *exchange(n_dev, 1),
            *exchange(n_dev, cap),
            pltpu.VMEM((n_px, GROUP, 640), jnp.float32),
            pltpu.VMEM((2, GROUP, 640), jnp.float32),
            pltpu.VMEM((GROUP, LANES), jnp.float32),
            *exchange(n_dev, 16),
            *exchange(n_dev, 16),
            *exchange(n_dev, cap),
            pltpu.VMEM((2 * n_px * GROUP, 2 * HALF * KEPT), jnp.float32),
            pltpu.VMEM((2, 2 * CXP * CYP, NZP // 2), jnp.bfloat16),
            pltpu.VMEM((n_dev * cap, CXP * CYP * NZP // LANES), jnp.bfloat16),
            pltpu.SemaphoreType.DMA((7,)),
            pltpu.SemaphoreType.DMA((5,)),
            pltpu.SemaphoreType.DMA((6,)),
            pltpu.SemaphoreType.DMA((6, 2)),
        ],
        compiler_params=pltpu.CompilerParams(
            collective_id=0, has_side_effects=True, vmem_limit_bytes=64 * 1024 * 1024
        ),
    )(charge, dest.reshape(1, slots), local_ids.reshape(1, slots), green_hat, *tables)


def solution(mesh):
    planes = mesh.shape["px"] == 4 and mesh.shape["pz"] == 8
    return jax.shard_map(
        local_fused if planes else local,
        mesh=mesh,
        in_specs=(
            P(AXES, None),
            P(AXES, None),
            P(AXES),
            P(None, "px", "pz"),
        ),
        out_specs=P(AXES, None),
        check_vma=False,
    )
```
